32 devices in a mesh: slab: 8 (over z, y), dom: 4 (over x, core).
Axes of the slice: x: 2, y: 2, z: 4, core: 2. Of those that a mesh axis runs over, the one named last changes fastest.
Arguments:
- atom_features: bfloat16 [4096, 3200], P(('slab', 'dom')), may hold values from -6 to 6
- halo_lists: int32 [8, 32, 8], P(None, ('slab', 'dom')), may hold values from 0 to 127, as said below
- probe_atoms: int32 [8, 8192], P(None, ('slab', 'dom')), may hold values from -1 to 255, as said below
- offsets: float32 [3, 8, 8192], P(None, None, ('slab', 'dom')), may hold values from -4 to 4, as said below
- radial_weights: float32 [8, 640], replicated, may hold values from -4 to 4
- probe_weight: float32 [128, 128], replicated, may hold values from -0.5 to 0.5
- out_weight: float32 [128], replicated, may hold values from -0.5 to 0.5
- density_cotangent: float32 [8192], P(('slab', 'dom')), may hold values from -6 to 6
Outputs:
- density: float32 [8192], P(('slab', 'dom'))
- atom_grads: float32 [4096, 3200], P(('slab', 'dom'))
The draws below stay inside these ranges and needn't reach their ends.
Inputs may be any that keep to these rules, and one draw needn't show every extreme that they name: `halo_lists`: within one slab and one owner the listed local atom numbers are distinct. `probe_atoms`: -1 marks an empty slot; any other entry is a row of the probe's slab table of 256 rows. Row t belongs to owner t // 8. Among the slots of the probes of one device, at most 64 live ones name rows of one owner; in every draw some owner is named by exactly 64 live slots from every device. `offsets`: every displacement has a length between 0.5 and 4.
All inputs are finite; a program needn't handle non-finite values.
Results may differ from the reference program's by a relative error of at most 0.0041.
Values may be sent and summed in bfloat16 or wider, within the bound.
No kernel may reach another device: no remote copies, remote signals or barrier semaphores. Data moves between devices by JAX's collectives and lax.ppermute only.
A program may use at most 128 MiB of HBM per device.

```python
import jax
import jax.numpy as jnp
from jax import lax

C = 128
NB = 8
K = 8
HSLOT = 8
A_DEV = 128
P_DEV = 256
ATOMS = 4096
PROBES = 8192
N_SLAB = 8
N_DOM = 4
DEVICES = 32


def draw_halo_lists(key, part):
    scores = jax.random.randint(jax.random.fold_in(key, 11), (N_SLAB, DEVICES, A_DEV), 0, 2 ** 20)
    scores = scores * A_DEV + jnp.arange(A_DEV)[None, None, :]
    order = jnp.argsort(scores, axis=-1, stable=True)
    return order[:, :, :HSLOT].astype(jnp.int32)


def draw_probe_atoms(key, part):
    base = jax.random.fold_in(key, 23)
    key_full, key_count, key_score, key_pick = jax.random.split(base, 4)
    total = K * P_DEV
    cap = total // DEVICES
    full_owner = jax.random.randint(key_full, (), 0, DEVICES)
    counts = jax.random.randint(key_count, (DEVICES, DEVICES), max(cap // 4, 1), cap + 1)
    counts = jnp.where(jnp.arange(DEVICES)[None, :] == full_owner, cap, counts)
    bounds = jnp.cumsum(counts, axis=1).astype(jnp.int32)
    ranks = jnp.arange(total).astype(jnp.int32)
    owner_of_rank = jax.vmap(lambda edge: jnp.searchsorted(edge, ranks, side='right'))(bounds).astype(jnp.int32)
    scores = jax.random.randint(key_score, (DEVICES, total), 0, 2 ** 14) * total + ranks[None, :]
    order = jnp.argsort(scores, axis=1)
    owner_pos = jax.vmap(lambda place, owner: jnp.zeros((total,), jnp.int32).at[place].set(owner))(order, owner_of_rank)
    picks = jax.random.randint(key_pick, (DEVICES, total), 0, HSLOT)
    rows = jnp.where(owner_pos < DEVICES, owner_pos * HSLOT + picks, -1)
    return rows.reshape(DEVICES, K, P_DEV).transpose(1, 0, 2).reshape(K, PROBES).astype(jnp.int32)


def draw_offsets(key, part):
    key_z, key_phi, key_len = jax.random.split(jax.random.fold_in(key, 37), 3)
    zpart = jax.random.uniform(key_z, (K, PROBES), jnp.float32, -1.0, 1.0)
    phi = jax.random.uniform(key_phi, (K, PROBES), jnp.float32, 0.0, 6.2831853)
    length = jax.random.uniform(key_len, (K, PROBES), jnp.float32, 0.5, 4.0)
    radius = jnp.sqrt(jnp.maximum(1.0 - zpart * zpart, 0.0))
    return jnp.stack([length * radius * jnp.cos(phi), length * radius * jnp.sin(phi), length * zpart]).astype(jnp.float32)


def level_of(stream_key, extent, cuts, low, largest):
    loudness = 1.0
    for axis_at, blocks in cuts:
        heights = jax.random.uniform(jax.random.fold_in(jax.random.fold_in(stream_key, 6), axis_at), (blocks,), jnp.float32, low / len(cuts), largest / len(cuts))
        loudness = loudness * jnp.repeat(jnp.exp(heights), extent[axis_at] // blocks).reshape((-1,) + (1,) * (len(extent) - 1 - axis_at))
    return loudness


def gaussian(own_key, shape, width, bound, cuts=(), kind=jnp.bfloat16):
    result = jax.random.normal(own_key, shape, jnp.float32) * width
    if len(cuts) > 0:
        result = level_of(own_key, shape, cuts, -0.22, 0.18) * result
    return jnp.clip(result, min=-bound, max=bound).astype(kind)


def setup_inputs(seed: int = 0) -> dict:
    splits = jax.random.split(jax.random.key(seed), 9)
    return {
        "atom_features": gaussian(splits[0], (ATOMS, 25 * C), 1.0, 6.0, ((0, 32),)),
        "halo_lists": draw_halo_lists(jax.random.fold_in(splits[8], 71), 0),
        "probe_atoms": draw_probe_atoms(jax.random.fold_in(splits[8], 71), 0),
        "offsets": draw_offsets(jax.random.fold_in(splits[8], 71), 0),
        "radial_weights": gaussian(splits[4], (NB, 5 * C), 0.7, 4.0, (), jnp.float32),
        "probe_weight": gaussian(splits[5], (C, C), C ** -0.5, 0.5, (), jnp.float32),
        "out_weight": gaussian(splits[6], (C,), C ** -0.5, 0.5, (), jnp.float32),
        "density_cotangent": gaussian(splits[7], (PROBES,), 1.0, 6.0, ((0, 32),), jnp.float32),
    }


cutoff_radius = 4.0
probe_block = 64

def harmonics(xcoord, ycoord, zcoord):
    xsq = xcoord * xcoord
    ysq = ycoord * ycoord
    zsq = zcoord * zcoord
    values = [0.28209479 * jnp.ones_like(xcoord), 0.48860251 * ycoord, 0.48860251 * zcoord, 0.48860251 * xcoord, 1.09254843 * xcoord * ycoord, 1.09254843 * ycoord * zcoord, 0.31539157 * (3.0 * zsq - 1.0), 1.09254843 * xcoord * zcoord, 0.54627422 * (xsq - ysq), 0.59004359 * ycoord * (3.0 * xsq - ysq), 2.89061144 * xcoord * ycoord * zcoord, 0.4570458 * ycoord * (5.0 * zsq - 1.0), 0.37317633 * zcoord * (5.0 * zsq - 3.0), 0.4570458 * xcoord * (5.0 * zsq - 1.0), 1.44530572 * zcoord * (xsq - ysq), 0.59004359 * xcoord * (xsq - 3.0 * ysq), 2.50334294 * xcoord * ycoord * (xsq - ysq), 1.77013077 * ycoord * zcoord * (3.0 * xsq - ysq), 0.9461747 * xcoord * ycoord * (7.0 * zsq - 1.0), 0.66904654 * ycoord * zcoord * (7.0 * zsq - 3.0), 0.10578555 * (35.0 * zsq * zsq - 30.0 * zsq + 3.0), 0.66904654 * xcoord * zcoord * (7.0 * zsq - 3.0), 0.47308735 * (xsq - ysq) * (7.0 * zsq - 1.0), 1.77013077 * xcoord * zcoord * (xsq - 3.0 * ysq), 0.62583574 * (xsq * (xsq - 3.0 * ysq) - ysq * (3.0 * xsq - ysq))]
    return jnp.stack(values, axis=-1)

def geometry(offset_block, radial_weights):
    length = jnp.sqrt(lax.optimization_barrier(jnp.sum(offset_block * offset_block, axis=0)))
    orders = jnp.arange(1, radial_weights.shape[0] + 1).astype(length.dtype)
    envelope = 0.5 * (jnp.cos(jnp.pi * length / cutoff_radius) + 1.0)
    basis = jnp.sqrt(2.0 / cutoff_radius) * jnp.sin(orders * jnp.pi * length[..., None] / cutoff_radius) / length[..., None] * envelope[..., None]
    slots, probes = length.shape
    channels = radial_weights.shape[1] // 5
    radial = jnp.dot(basis.reshape(-1, basis.shape[-1]), radial_weights, precision=lax.Precision.HIGHEST).reshape(slots, probes, 5, channels)
    unit = offset_block / length[None]
    harmonic = harmonics(unit[0], unit[1], unit[2]).astype(jnp.bfloat16)
    return (radial, harmonic)

def probe_pass(gathered, alive_mask, offset_block, radial_weights, probe_weight, out_weight, cot_block):
    radial, harmonic = geometry(offset_block, radial_weights)
    summed = jnp.zeros((gathered.shape[1], gathered.shape[3]), jnp.float32)
    for degree in range(5):
        part_y = harmonic[:, :, degree * degree:(degree + 1) ** 2].astype(jnp.float32)
        part_h = gathered[:, :, degree * degree:(degree + 1) ** 2, :].astype(jnp.float32)
        contracted = jnp.einsum('kpm,kpmc->kpc', part_y, part_h)
        summed = summed + lax.optimization_barrier(jnp.sum(radial[:, :, degree] * contracted * alive_mask[..., None], axis=0))
    preact = jnp.dot(summed, probe_weight, precision=lax.Precision.HIGHEST)
    density = jnp.dot(jax.nn.silu(preact), out_weight, precision=lax.Precision.HIGHEST)
    sigma = jax.nn.sigmoid(preact)
    dpre = cot_block[:, None] * out_weight[None, :] * sigma * (1.0 + preact * (1.0 - sigma))
    dsum = jnp.dot(dpre, probe_weight.T, precision=lax.Precision.HIGHEST)
    weighted = alive_mask[..., None] * dsum[None]
    pieces = []
    for degree in range(5):
        part_y = harmonic[:, :, degree * degree:(degree + 1) ** 2].astype(jnp.float32)
        pieces.append(part_y[..., None] * (weighted * radial[:, :, degree])[:, :, None, :])
    row_grads = jnp.concatenate(pieces, axis=2)
    return (density, row_grads.reshape(gathered.shape[0], gathered.shape[1], -1))

def reference(atom_features, halo_lists, probe_atoms, offsets, radial_weights, probe_weight, out_weight, density_cotangent):
    owners = (jnp.arange(DEVICES).astype(jnp.int32) * A_DEV)[None, :, None]
    global_rows = (owners + halo_lists.astype(jnp.int32)).reshape(N_SLAB, DEVICES * HSLOT)
    count = PROBES // probe_block
    feature_len = 25 * C

    def step(grads, number):
        start = (number * probe_block).astype(jnp.int32)
        slab_now = start // (N_DOM * P_DEV)
        index_block = lax.dynamic_slice_in_dim(probe_atoms, start, probe_block, 1)
        alive_mask = (index_block >= 0).astype(jnp.float32)
        slot_index = jnp.maximum(index_block, 0)
        row_ids = lax.dynamic_index_in_dim(global_rows, slab_now, 0, keepdims=False)[slot_index]
        gathered = atom_features[row_ids.reshape(-1)].reshape(K, probe_block, 25, C)
        offset_block = lax.dynamic_slice_in_dim(offsets, start, probe_block, 2)
        cot_block = lax.dynamic_slice_in_dim(density_cotangent, start, probe_block, 0)
        density, row_grads = probe_pass(gathered, alive_mask, offset_block, radial_weights, probe_weight, out_weight, cot_block)
        grads = grads.at[row_ids.reshape(-1)].add(row_grads.reshape(-1, feature_len))
        return (grads, density)
    grads, blocks = lax.scan(step, jnp.zeros((ATOMS, feature_len), jnp.float32), jnp.arange(count).astype(jnp.int32))
    return (blocks.reshape(PROBES), grads)
```

```python
import functools

import jax
import jax.numpy as jnp
from jax import lax
from jax.experimental import pallas as pl
from jax.experimental.pallas import tpu as pltpu
from jax.sharding import PartitionSpec as P

cutoff_radius = 4.0
COMPONENTS = 25
BF = jnp.bfloat16
F32 = jnp.float32
VMEM_LIMIT = 50 * 1024 * 1024


def iota(shape, dim):
    return lax.broadcasted_iota(jnp.int32, shape, dim)


def dot_nn(a, b):
    return lax.dot_general(a, b, (((1,), (0,)), ((), ())), preferred_element_type=F32)


def dot_nt(a, b):
    return lax.dot_general(a, b, (((1,), (1,)), ((), ())), preferred_element_type=F32)


def dot_tn(a, b):
    return lax.dot_general(a, b, (((0,), (0,)), ((), ())), preferred_element_type=F32)


def split(value):
    high = value.astype(BF)
    return high, (value - high.astype(F32)).astype(BF)


def harmonic_rows(xc, yc, zc):
    xsq = xc * xc
    ysq = yc * yc
    zsq = zc * zc
    return [
        0.28209479 * jnp.ones_like(xc),
        0.48860251 * yc,
        0.48860251 * zc,
        0.48860251 * xc,
        1.09254843 * xc * yc,
        1.09254843 * yc * zc,
        0.31539157 * (3.0 * zsq - 1.0),
        1.09254843 * xc * zc,
        0.54627422 * (xsq - ysq),
        0.59004359 * yc * (3.0 * xsq - ysq),
        2.89061144 * xc * yc * zc,
        0.4570458 * yc * (5.0 * zsq - 1.0),
        0.37317633 * zc * (5.0 * zsq - 3.0),
        0.4570458 * xc * (5.0 * zsq - 1.0),
        1.44530572 * zc * (xsq - ysq),
        0.59004359 * xc * (xsq - 3.0 * ysq),
        2.50334294 * xc * yc * (xsq - ysq),
        1.77013077 * yc * zc * (3.0 * xsq - ysq),
        0.9461747 * xc * yc * (7.0 * zsq - 1.0),
        0.66904654 * yc * zc * (7.0 * zsq - 3.0),
        0.10578555 * (35.0 * zsq * zsq - 30.0 * zsq + 3.0),
        0.66904654 * xc * zc * (7.0 * zsq - 3.0),
        0.47308735 * (xsq - ysq) * (7.0 * zsq - 1.0),
        1.77013077 * xc * zc * (xsq - 3.0 * ysq),
        0.62583574 * (xsq * (xsq - 3.0 * ysq) - ysq * (3.0 * xsq - ysq)),
    ]


def owner_onehot(halo, rows, atoms, hslot):
    n_slab = halo.shape[0]
    pick = (iota((rows, n_slab), 0) // hslot == iota((rows, n_slab), 1)).astype(BF)
    spread = dot_nn(pick, halo.astype(BF))
    mine = iota((rows, hslot), 0) % hslot == iota((rows, hslot), 1)
    column = jnp.sum(jnp.where(mine, spread, 0.0), axis=1, keepdims=True).astype(jnp.int32)
    return (iota((rows, atoms), 1) == column).astype(BF)


def pack_kernel(parts, h_ref, halo_ref, out_ref):
    n_slab, hslot = halo_ref.shape[0], halo_ref.shape[2]
    rows = n_slab * hslot
    onehot = owner_onehot(halo_ref[:, 0, :].astype(F32), rows, h_ref.shape[0], hslot)
    quarter = 128 // parts
    lane_part = iota((rows, 128), 1) // quarter
    groups = -(-COMPONENTS // parts)
    for group in range(groups):
        members = min(parts, COMPONENTS - group * parts)
        chosen = dot_nn(onehot, h_ref[:, group * parts * 128 : (group * parts + members) * 128])
        blocks = []
        for part in range(parts):
            total = jnp.zeros((rows, 128), F32)
            for i in range(members):
                source = chosen[:, i * 128 : (i + 1) * 128]
                shift = ((i - part) * quarter) % 128
                if shift:
                    source = pltpu.roll(source, shift, 1)
                total = jnp.where(lane_part == i, source, total)
            blocks.append(total.reshape(n_slab, hslot, 128))
        stacked = jnp.stack(blocks, axis=1).reshape(n_slab * parts * hslot, 128)
        out_ref[:, group * 128 : (group + 1) * 128] = stacked.astype(BF)


def unpack_kernel(parts, recv_ref, halo_ref, out_ref):
    n_slab, hslot = halo_ref.shape[0], halo_ref.shape[2]
    rows = n_slab * hslot
    onehot = owner_onehot(halo_ref[:, 0, :].astype(F32), rows, out_ref.shape[0], hslot)
    turned = onehot.astype(F32).T.astype(BF)
    quarter = 128 // parts
    lane_part = iota((rows, 128), 1) // quarter
    groups = -(-COMPONENTS // parts)
    for group in range(groups):
        members = min(parts, COMPONENTS - group * parts)
        got = recv_ref[:, group * 128 : (group + 1) * 128].astype(F32)
        got = got.reshape(n_slab, parts, hslot, 128)
        pieces = [got[:, part].reshape(rows, 128) for part in range(parts)]
        for i in range(members):
            total = jnp.zeros((rows, 128), F32)
            for part in range(parts):
                shift = ((part - i) * quarter) % 128
                source = pltpu.roll(pieces[part], shift, 1) if shift else pieces[part]
                total = jnp.where(lane_part == part, source, total)
            at = (group * parts + i) * 128
            out_ref[:, at : at + 128] = dot_nn(turned, total.astype(BF))


def basis_kernel(
    parts, channels, slots, probes, table,
    me_ref, *refs,
):
    blocks = refs[:parts]
    weight_ref = refs[parts]
    y_out, r_out, hot_out, turned_out, cot_out = refs[parts + 1 : parts + 6]
    geo, y_all, b_all, w_all = refs[parts + 6 :]
    k = pl.program_id(0)
    quarter = channels // parts
    orders = weight_ref.shape[0]

    @pl.when(k == 0)
    def _():
        me = me_ref[0]
        for j in range(parts):
            at = pl.multiple_of((me ^ j) * probes, 128)
            geo[:, pl.ds(at, probes)] = blocks[j][...]
        xo, yo, zo = (geo[i * slots : (i + 1) * slots, :] for i in range(3))
        length = jnp.sqrt(xo * xo + yo * yo + zo * zo)
        angle = jnp.pi * length / cutoff_radius
        sine, cosine = jnp.sin(angle), jnp.cos(angle)
        scale = (2.0 / cutoff_radius) ** 0.5 * (0.5 * (cosine + 1.0)) / length
        before, now = jnp.zeros_like(sine), sine
        high, low = [], []
        for _n in range(orders):
            one, two = split(now * scale)
            high.append(one.astype(F32))
            low.append(two.astype(F32))
            before, now = now, 2.0 * cosine * now - before
        size = orders * slots
        top = jnp.concatenate(high, axis=0).astype(BF)
        b_all[0:size, :] = top
        b_all[size : 2 * size, :] = top
        b_all[2 * size : 3 * size, :] = jnp.concatenate(low, axis=0).astype(BF)
        y_all[...] = jnp.zeros_like(y_all)
        unit = (xo / length, yo / length, zo / length)
        for index, row in enumerate(harmonic_rows(*unit)):
            row = row.astype(BF).astype(F32)
            for slot in range(slots):
                y_all[slot * 32 + index : slot * 32 + index + 1, :] = row[slot : slot + 1, :]
        cot_out[...] = geo[4 * slots : 5 * slots, :]
        weights = weight_ref[...]
        w_high, w_low = split(weights)
        w_high, w_low = w_high.astype(F32), w_low.astype(F32)
        spread = []
        for source in (w_high, w_low, w_high):
            for n in range(orders):
                spread.append(jnp.broadcast_to(source[n : n + 1, :], (slots, 5 * channels)))
        spread = jnp.concatenate(spread, axis=0).astype(BF)
        row = iota((5 * quarter, 5 * channels), 0)
        wanted = row // quarter * channels + me * quarter + row % quarter
        choose = (iota((5 * quarter, 5 * channels), 1) == wanted).astype(BF)
        w_all[...] = dot_nt(choose, spread)

    lane = iota(w_all.shape, 1)
    mine = jnp.where(lane % slots == k, w_all[...], 0.0).astype(BF)
    r_out[0] = dot_nn(mine, b_all[...])
    y_out[0] = y_all[pl.ds(pl.multiple_of(k * 32, 32), 32), :]
    atoms = geo[pl.ds(3 * slots + k, 1), :].astype(jnp.int32)
    hot = (iota((table, parts * probes), 0) == atoms).astype(F32)
    hot_out[0] = hot.astype(BF)
    turned_out[0] = hot.T.astype(BF)


def forward_kernel(quarter, h_ref, hot_ref, y_ref, r_ref, s_ref, turned, total):
    k = pl.program_id(0)

    @pl.when(k == 0)
    def _():
        turned[...] = h_ref[...].astype(F32).T.astype(BF)
        total[...] = jnp.zeros_like(total)

    width = total.shape[1]
    step = 256
    for at in range(0, width, step):
        lanes = slice(at, at + step)
        hot = hot_ref[0, :, lanes]
        acc = total[:, lanes]
        for degree in range(5):
            first, last = degree * degree, (degree + 1) ** 2
            got = dot_nn(turned[first * quarter : last * quarter, :], hot)
            inner = got[0:quarter] * y_ref[0, first : first + 1, lanes]
            for m in range(1, last - first):
                inner = inner + (
                    got[m * quarter : (m + 1) * quarter]
                    * y_ref[0, first + m : first + m + 1, lanes]
                )
            acc = acc + inner * r_ref[0, degree * quarter : (degree + 1) * quarter, lanes]
        total[:, lanes] = acc

    @pl.when(k == pl.num_programs(0) - 1)
    def _():
        s_ref[...] = total[...].astype(BF)


def backward_kernel(
    parts, quarter, probes,
    me_ref, *refs,
):
    sums = refs[:parts]
    pw_ref, ow_ref, cot_ref, turned_ref, y_ref, r_ref = refs[parts : parts + 6]
    grads_ref, density_ref = refs[parts + 6 : parts + 8]
    s_all, ds, z, acc, dens = refs[parts + 8 :]
    k = pl.program_id(0)
    me = me_ref[0]
    channels = parts * quarter

    @pl.when(k == 0)
    def _():
        for j in range(parts):
            at = pl.multiple_of((me ^ j) * quarter, quarter)
            s_all[pl.ds(at, quarter), :] = sums[j][...].astype(F32)
        pw = pw_ref[...]
        p_high, p_low = split(pw)
        given = s_all[...].astype(BF)
        pre = dot_tn(p_high, given) + dot_tn(p_low, given)
        eye = iota((channels, channels), 0) == iota((channels, channels), 1)
        ow = jnp.sum(jnp.where(eye, ow_ref[...], 0.0), axis=1, keepdims=True)
        sigma = 1.0 / (1.0 + jnp.exp(-pre))
        dens[...] = jnp.sum(pre * sigma * ow, axis=0, keepdims=True)
        here = pl.multiple_of(me * probes, 128)
        density_ref[...] = dens[:, pl.ds(here, probes)]
        dpre = cot_ref[0:1, :] * ow * sigma * (1.0 + pre * (1.0 - sigma))
        d_high, d_low = split(dpre)
        own = pl.multiple_of(me * quarter, quarter)
        o_high, o_low = split(pw_ref[pl.ds(own, quarter), :])
        ds[...] = dot_nn(o_high, d_high) + dot_nn(o_high, d_low) + dot_nn(o_low, d_high)
        acc[...] = jnp.zeros_like(acc)

    for degree in range(5):
        first, last = degree * degree, (degree + 1) ** 2
        weighted = ds[...] * r_ref[0, degree * quarter : (degree + 1) * quarter, :]
        for m in range(first, last):
            z[m * quarter : (m + 1) * quarter, :] = (weighted * y_ref[0, m : m + 1, :]).astype(BF)
    acc[...] += dot_nn(z[...], turned_ref[0])

    @pl.when(k == pl.num_programs(0) - 1)
    def _():
        filled = (COMPONENTS * quarter) // 128 * 128
        grads_ref[:, 0:filled] = acc[0:filled, :].T.astype(BF)
        rest = acc[filled : COMPONENTS * quarter, :]
        space = grads_ref.shape[1] - COMPONENTS * quarter
        rest = jnp.concatenate([rest, jnp.zeros((space, rest.shape[1]), F32)], axis=0)
        grads_ref[:, filled:] = rest.T.astype(BF)


def whole(shape):
    return pl.BlockSpec(shape, lambda *_: (0,) * len(shape))


def spread_over(value, n_dom):
    blocks = {0: value}
    bit = n_dom // 2
    while bit:
        pairs = [(i, i ^ bit) for i in range(n_dom)]
        for j in list(blocks):
            blocks[j | bit] = lax.ppermute(blocks[j], "dom", pairs)
        bit //= 2
    return [blocks[j] for j in range(n_dom)]


def shards(
    atom_features,
    halo_lists,
    probe_atoms,
    offsets,
    radial_weights,
    probe_weight,
    out_weight,
    density_cotangent,
):
    n_slab = lax.axis_size("slab")
    n_dom = lax.axis_size("dom")
    atoms, feature_len = atom_features.shape
    channels = feature_len // COMPONENTS
    slots, probes = probe_atoms.shape
    hslot = halo_lists.shape[2]
    table = n_slab * n_dom * hslot
    quarter = channels // n_dom
    orders = radial_weights.shape[0]
    slab_probes = n_dom * probes
    packed = -(-COMPONENTS // n_dom) * 128
    me = lax.axis_index("dom").astype(jnp.int32).reshape(1)
    params = pltpu.CompilerParams(vmem_limit_bytes=VMEM_LIMIT)

    geometry = jnp.concatenate(
        [
            offsets.reshape(3 * slots, probes),
            probe_atoms.astype(F32),
            jnp.broadcast_to(density_cotangent[None, :], (slots, probes)),
        ],
        axis=0,
    )
    geo_blocks = spread_over(geometry, n_dom)

    send = pl.pallas_call(
        functools.partial(pack_kernel, n_dom),
        out_shape=jax.ShapeDtypeStruct((table, packed), BF),
        compiler_params=params,
        name="pack",
    )(atom_features, halo_lists)
    halo = lax.all_to_all(send, ("slab", "dom"), split_axis=0, concat_axis=0, tiled=True)

    y_all, r_all, hot, hot_turned, cot = pl.pallas_call(
        functools.partial(basis_kernel, n_dom, channels, slots, probes, table),
        grid_spec=pltpu.PrefetchScalarGridSpec(
            num_scalar_prefetch=1,
            grid=(slots,),
            in_specs=[whole(geometry.shape)] * n_dom + [whole(radial_weights.shape)],
            out_specs=[
                pl.BlockSpec((1, 32, slab_probes), lambda k, _: (k, 0, 0)),
                pl.BlockSpec((1, 5 * quarter, slab_probes), lambda k, _: (k, 0, 0)),
                pl.BlockSpec((1, table, slab_probes), lambda k, _: (k, 0, 0)),
                pl.BlockSpec((1, slab_probes, table), lambda k, _: (k, 0, 0)),
                whole((slots, slab_probes)),
            ],
            scratch_shapes=[
                pltpu.VMEM((5 * slots, slab_probes), F32),
                pltpu.VMEM((32 * slots, slab_probes), F32),
                pltpu.VMEM((3 * orders * slots, slab_probes), BF),
                pltpu.VMEM((5 * quarter, 3 * orders * slots), F32),
            ],
        ),
        out_shape=[
            jax.ShapeDtypeStruct((slots, 32, slab_probes), F32),
            jax.ShapeDtypeStruct((slots, 5 * quarter, slab_probes), F32),
            jax.ShapeDtypeStruct((slots, table, slab_probes), BF),
            jax.ShapeDtypeStruct((slots, slab_probes, table), BF),
            jax.ShapeDtypeStruct((slots, slab_probes), F32),
        ],
        compiler_params=params,
        name="basis",
    )(me, *geo_blocks, radial_weights)

    sums = pl.pallas_call(
        functools.partial(forward_kernel, quarter),
        grid=(slots,),
        in_specs=[
            whole((table, packed)),
            pl.BlockSpec((1, table, slab_probes), lambda k: (k, 0, 0)),
            pl.BlockSpec((1, 32, slab_probes), lambda k: (k, 0, 0)),
            pl.BlockSpec((1, 5 * quarter, slab_probes), lambda k: (k, 0, 0)),
        ],
        out_specs=whole((quarter, slab_probes)),
        out_shape=jax.ShapeDtypeStruct((quarter, slab_probes), BF),
        scratch_shapes=[
            pltpu.VMEM((packed * n_dom // 128 * quarter, table), BF),
            pltpu.VMEM((quarter, slab_probes), F32),
        ],
        compiler_params=params,
        name="forward",
    )(halo, hot, y_all, r_all)

    sum_blocks = spread_over(sums, n_dom)

    grads, density = pl.pallas_call(
        functools.partial(backward_kernel, n_dom, quarter, probes),
        grid_spec=pltpu.PrefetchScalarGridSpec(
            num_scalar_prefetch=1,
            grid=(slots,),
            in_specs=[whole((quarter, slab_probes))] * n_dom
            + [
                whole((channels, channels)),
                whole((1, channels)),
                whole((slots, slab_probes)),
                pl.BlockSpec((1, slab_probes, table), lambda k, _: (k, 0, 0)),
                pl.BlockSpec((1, 32, slab_probes), lambda k, _: (k, 0, 0)),
                pl.BlockSpec((1, 5 * quarter, slab_probes), lambda k, _: (k, 0, 0)),
            ],
            out_specs=[whole((table, packed)), whole((1, probes))],
            scratch_shapes=[
                pltpu.VMEM((channels, slab_probes), F32),
                pltpu.VMEM((quarter, slab_probes), F32),
                pltpu.VMEM((COMPONENTS * quarter, slab_probes), BF),
                pltpu.VMEM((COMPONENTS * quarter, table), F32),
                pltpu.VMEM((1, slab_probes), F32),
            ],
        ),
        out_shape=[
            jax.ShapeDtypeStruct((table, packed), BF),
            jax.ShapeDtypeStruct((1, probes), F32),
        ],
        compiler_params=params,
        name="backward",
    )(me, *sum_blocks, probe_weight, out_weight.reshape(1, channels), cot, hot_turned, y_all, r_all)

    back = lax.all_to_all(grads, ("slab", "dom"), split_axis=0, concat_axis=0, tiled=True)
    atom_grads = pl.pallas_call(
        functools.partial(unpack_kernel, n_dom),
        out_shape=jax.ShapeDtypeStruct((atoms, feature_len), F32),
        compiler_params=params,
        name="unpack",
    )(back, halo_lists)
    return (density.reshape(probes), atom_grads)


def solution(mesh):
    return jax.shard_map(
        shards,
        mesh=mesh,
        in_specs=(
            P(("slab", "dom"), None),
            P(None, ("slab", "dom"), None),
            P(None, ("slab", "dom")),
            P(None, None, ("slab", "dom")),
            P(),
            P(),
            P(),
            P(("slab", "dom")),
        ),
        out_specs=(P(("slab", "dom")), P(("slab", "dom"), None)),
        check_vma=False,
    )
```

```python
import functools

import jax
import jax.numpy as jnp
from jax import lax
from jax.experimental import pallas as pl
from jax.experimental.pallas import tpu as pltpu
from jax.sharding import PartitionSpec as P

cutoff_radius = 4.0
COMPONENTS = 25
BF = jnp.bfloat16
F32 = jnp.float32


def iota(shape, dim):
    return lax.broadcasted_iota(jnp.int32, shape, dim)


def dot_nn(a, b):
    return lax.dot_general(a, b, (((1,), (0,)), ((), ())), preferred_element_type=F32)


def dot_nt(a, b):
    return lax.dot_general(a, b, (((1,), (1,)), ((), ())), preferred_element_type=F32)


def dot_tn(a, b):
    return lax.dot_general(a, b, (((0,), (0,)), ((), ())), preferred_element_type=F32)


def split(value):
    high = value.astype(BF)
    return high, (value - high.astype(F32)).astype(BF)


def harmonic_rows(xc, yc, zc):
    xsq = xc * xc
    ysq = yc * yc
    zsq = zc * zc
    return [
        0.28209479 * jnp.ones_like(xc),
        0.48860251 * yc,
        0.48860251 * zc,
        0.48860251 * xc,
        1.09254843 * xc * yc,
        1.09254843 * yc * zc,
        0.31539157 * (3.0 * zsq - 1.0),
        1.09254843 * xc * zc,
        0.54627422 * (xsq - ysq),
        0.59004359 * yc * (3.0 * xsq - ysq),
        2.89061144 * xc * yc * zc,
        0.4570458 * yc * (5.0 * zsq - 1.0),
        0.37317633 * zc * (5.0 * zsq - 3.0),
        0.4570458 * xc * (5.0 * zsq - 1.0),
        1.44530572 * zc * (xsq - ysq),
        0.59004359 * xc * (xsq - 3.0 * ysq),
        2.50334294 * xc * yc * (xsq - ysq),
        1.77013077 * yc * zc * (3.0 * xsq - ysq),
        0.9461747 * xc * yc * (7.0 * zsq - 1.0),
        0.66904654 * yc * zc * (7.0 * zsq - 3.0),
        0.10578555 * (35.0 * zsq * zsq - 30.0 * zsq + 3.0),
        0.66904654 * xc * zc * (7.0 * zsq - 3.0),
        0.47308735 * (xsq - ysq) * (7.0 * zsq - 1.0),
        1.77013077 * xc * zc * (xsq - 3.0 * ysq),
        0.62583574 * (xsq * (xsq - 3.0 * ysq) - ysq * (3.0 * xsq - ysq)),
    ]


def owner_onehot(halo, rows, atoms, hslot):
    n_slab = halo.shape[0]
    pick = (iota((rows, n_slab), 0) // hslot == iota((rows, n_slab), 1)).astype(BF)
    spread = dot_nn(pick, halo.astype(BF))
    mine = iota((rows, hslot), 0) % hslot == iota((rows, hslot), 1)
    column = jnp.sum(jnp.where(mine, spread, 0.0), axis=1, keepdims=True).astype(jnp.int32)
    return (iota((rows, atoms), 1) == column).astype(BF)


def pack_kernel(
    parts,
    h_hbm, halo_hbm, off_hbm, atoms_hbm, cot_hbm,
    out_ref, geo_ref,
    h_ref, halo_ref, off_ref, atoms_ref, cot_ref, sems,
):
    groups = -(-COMPONENTS // parts)
    small = [(halo_hbm, halo_ref), (off_hbm, off_ref), (atoms_hbm, atoms_ref), (cot_hbm, cot_ref)]
    copies = [
        pltpu.make_async_copy(source, target, sems.at[i]) for i, (source, target) in enumerate(small)
    ]
    for group in range(groups):
        lanes = slice(group * parts * 128, min((group + 1) * parts, COMPONENTS) * 128)
        copies.append(
            pltpu.make_async_copy(h_hbm.at[:, lanes], h_ref.at[:, lanes], sems.at[4 + group])
        )
    for copy in copies:
        copy.start()
    for copy in copies[:4]:
        copy.wait()
    slots = atoms_ref.shape[0]
    for i in range(3):
        geo_ref[i * slots : (i + 1) * slots, :] = off_ref[i]
    geo_ref[3 * slots : 4 * slots, :] = atoms_ref[...].astype(F32)
    geo_ref[4 * slots : 5 * slots, :] = jnp.broadcast_to(cot_ref[...], atoms_ref.shape)
    n_slab, hslot = halo_ref.shape[0], halo_ref.shape[2]
    rows = n_slab * hslot
    onehot = owner_onehot(halo_ref[:, 0, :].astype(F32), rows, h_ref.shape[0], hslot)
    quarter = 128 // parts
    lane_part = iota((rows, 128), 1) // quarter
    for group in range(groups):
        copies[4 + group].wait()
        members = min(parts, COMPONENTS - group * parts)
        chosen = dot_nn(onehot, h_ref[:, group * parts * 128 : (group * parts + members) * 128])
        blocks = []
        for part in range(parts):
            total = jnp.zeros((rows, 128), F32)
            for i in range(members):
                source = chosen[:, i * 128 : (i + 1) * 128]
                shift = ((i - part) * quarter) % 128
                if shift:
                    source = pltpu.roll(source, shift, 1)
                total = jnp.where(lane_part == i, source, total)
            blocks.append(total.reshape(n_slab, hslot, 128))
        stacked = jnp.stack(blocks, axis=1).reshape(n_slab * parts * hslot, 128)
        out_ref[:, group * 128 : (group + 1) * 128] = stacked.astype(BF)


def unpack_kernel(parts, recv_ref, halo_ref, out_hbm, out_ref, sems):
    n_slab, hslot = halo_ref.shape[0], halo_ref.shape[2]
    rows = n_slab * hslot
    onehot = owner_onehot(halo_ref[:, 0, :].astype(F32), rows, out_ref.shape[0], hslot)
    turned = onehot.astype(F32).T.astype(BF)
    quarter = 128 // parts
    lane_part = iota((rows, 128), 1) // quarter
    groups = -(-COMPONENTS // parts)
    copies = []
    for group in range(groups):
        members = min(parts, COMPONENTS - group * parts)
        got = recv_ref[:, group * 128 : (group + 1) * 128].astype(F32)
        got = got.reshape(n_slab, parts, hslot, 128)
        pieces = [got[:, part].reshape(rows, 128) for part in range(parts)]
        for i in range(members):
            total = jnp.zeros((rows, 128), F32)
            for part in range(parts):
                shift = ((part - i) * quarter) % 128
                source = pltpu.roll(pieces[part], shift, 1) if shift else pieces[part]
                total = jnp.where(lane_part == part, source, total)
            at = (group * parts + i) * 128
            out_ref[:, at : at + 128] = dot_nn(turned, total.astype(BF))
        lanes = slice(group * parts * 128, (group * parts + members) * 128)
        copy = pltpu.make_async_copy(out_ref.at[:, lanes], out_hbm.at[:, lanes], sems.at[group])
        copy.start()
        copies.append(copy)
    for copy in copies:
        copy.wait()


def basis_kernel(
    parts, channels, slots, probes,
    me_ref, *refs,
):
    blocks = refs[:parts]
    weight_ref = refs[parts]
    y_all, cot_out, atoms_out, b_all, w_all, geo = refs[parts + 1 :]
    quarter = channels // parts
    orders = weight_ref.shape[0]
    me = me_ref[0]
    for j in range(parts):
        at = pl.multiple_of((me ^ j) * probes, 128)
        geo[:, pl.ds(at, probes)] = blocks[j][...]
    xo, yo, zo = (geo[i * slots : (i + 1) * slots, :] for i in range(3))
    length = jnp.sqrt(xo * xo + yo * yo + zo * zo)
    angle = jnp.pi * length / cutoff_radius
    sine, cosine = jnp.sin(angle), jnp.cos(angle)
    scale = (2.0 / cutoff_radius) ** 0.5 * (0.5 * (cosine + 1.0)) / length
    before, now = jnp.zeros_like(sine), sine
    high, low = [], []
    for _n in range(orders):
        one, two = split(now * scale)
        high.append(one.astype(F32))
        low.append(two.astype(F32))
        before, now = now, 2.0 * cosine * now - before
    size = orders * slots
    top = jnp.concatenate(high, axis=0).astype(BF)
    b_all[0:size, :] = top
    b_all[size : 2 * size, :] = top
    b_all[2 * size : 3 * size, :] = jnp.concatenate(low, axis=0).astype(BF)
    unit = (xo / length, yo / length, zo / length)
    for index, row in enumerate(harmonic_rows(*unit)):
        row = row.astype(BF).astype(F32)
        for slot in range(slots):
            y_all[slot, index : index + 1, :] = row[slot : slot + 1, :]
    cot_out[...] = geo[4 * slots : 5 * slots, :]
    atoms_out[...] = geo[3 * slots : 4 * slots, :].astype(jnp.int32)
    weights = weight_ref[...]
    w_high, w_low = split(weights)
    w_high, w_low = w_high.astype(F32), w_low.astype(F32)
    spread = []
    for source in (w_high, w_low, w_high):
        for n in range(orders):
            spread.append(jnp.broadcast_to(source[n : n + 1, :], (slots, 5 * channels)))
    spread = jnp.concatenate(spread, axis=0).astype(BF)
    row = iota((5 * quarter, 5 * channels), 0)
    wanted = row // quarter * channels + me * quarter + row % quarter
    choose = (iota((5 * quarter, 5 * channels), 1) == wanted).astype(BF)
    w_all[...] = dot_nt(choose, spread)


def radial(k, slots, w_ref, b_ref, lanes):
    weights = w_ref[...]
    mine = jnp.where(iota(weights.shape, 1) % slots == k, weights, 0.0).astype(BF)
    return dot_nn(mine, b_ref[:, lanes])


def onehot_of(k, atoms_ref, table, lanes):
    atoms = atoms_ref[k : k + 1, lanes]
    return (iota((table, atoms.shape[1]), 0) == atoms).astype(F32).astype(BF)


def forward_kernel(
    quarter, h_ref, y_ref, atoms_ref, b_ref, w_ref, s_ref, hot_ref, r_ref, turned, total
):
    slots, table = atoms_ref.shape[0], h_ref.shape[0]
    turned[...] = h_ref[...].astype(F32).T.astype(BF)
    total[...] = jnp.zeros_like(total)
    width = total.shape[1]
    step = 256

    for k in range(slots):
        for at in range(0, width, step):
            lanes = slice(at, at + step)
            hot = onehot_of(k, atoms_ref, table, lanes)
            rad = radial(k, slots, w_ref, b_ref, lanes)
            hot_ref[k, :, lanes] = hot
            r_ref[k, :, lanes] = rad
            got = dot_nn(turned[0 : COMPONENTS * quarter, :], hot)
            acc = total[:, lanes]
            for degree in range(5):
                first, last = degree * degree, (degree + 1) ** 2
                inner = got[first * quarter : (first + 1) * quarter] * y_ref[k, first : first + 1, lanes]
                for m in range(first + 1, last):
                    inner = inner + (
                        got[m * quarter : (m + 1) * quarter] * y_ref[k, m : m + 1, lanes]
                    )
                acc = acc + inner * rad[degree * quarter : (degree + 1) * quarter]
            total[:, lanes] = acc
    s_ref[...] = total[...].astype(BF)


def backward_kernel(
    parts, quarter, probes,
    me_ref, *refs,
):
    sums = refs[:parts]
    pw_ref, ow_ref, cot_ref, y_ref, hot_ref, r_ref = refs[parts : parts + 6]
    grads_ref, density_ref, s_all, ds, z, acc, dens = refs[parts + 6 :]
    slots = y_ref.shape[0]
    me = me_ref[0]
    channels = parts * quarter
    for j in range(parts):
        at = pl.multiple_of((me ^ j) * quarter, quarter)
        s_all[pl.ds(at, quarter), :] = sums[j][...].astype(F32)
    pw = pw_ref[...]
    p_high, p_low = split(pw)
    given = s_all[...].astype(BF)
    pre = dot_tn(p_high, given) + dot_tn(p_low, given)
    eye = iota((channels, channels), 0) == iota((channels, channels), 1)
    ow = jnp.sum(jnp.where(eye, ow_ref[...], 0.0), axis=1, keepdims=True)
    sigma = 1.0 / (1.0 + jnp.exp(-pre))
    dens[...] = jnp.sum(pre * sigma * ow, axis=0, keepdims=True)
    here = pl.multiple_of(me * probes, 128)
    density_ref[...] = dens[:, pl.ds(here, probes)]
    dpre = cot_ref[0:1, :] * ow * sigma * (1.0 + pre * (1.0 - sigma))
    d_high, d_low = split(dpre)
    own = pl.multiple_of(me * quarter, quarter)
    o_high, o_low = split(pw_ref[pl.ds(own, quarter), :])
    ds[...] = dot_nn(o_high, d_high) + dot_nn(o_high, d_low) + dot_nn(o_low, d_high)
    acc[...] = jnp.zeros_like(acc)

    for k in range(slots):
        for degree in range(5):
            first, last = degree * degree, (degree + 1) ** 2
            weighted = ds[...] * r_ref[k, degree * quarter : (degree + 1) * quarter, :]
            for m in range(first, last):
                z[m * quarter : (m + 1) * quarter, :] = (
                    weighted * y_ref[k, m : m + 1, :]
                ).astype(BF)
        acc[...] += dot_nt(z[...], hot_ref[k])

    filled = (COMPONENTS * quarter) // 128 * 128
    grads_ref[:, 0:filled] = acc[0:filled, :].T.astype(BF)
    rest = acc[filled : COMPONENTS * quarter, :]
    space = grads_ref.shape[1] - COMPONENTS * quarter
    rest = jnp.concatenate([rest, jnp.zeros((space, rest.shape[1]), F32)], axis=0)
    grads_ref[:, filled:] = rest.T.astype(BF)


def spread_over(value, n_dom):
    blocks = {0: value}
    bit = n_dom // 2
    while bit:
        pairs = [(i, i ^ bit) for i in range(n_dom)]
        for j in list(blocks):
            blocks[j | bit] = lax.ppermute(blocks[j], "dom", pairs)
        bit //= 2
    return [blocks[j] for j in range(n_dom)]


def shards(
    atom_features,
    halo_lists,
    probe_atoms,
    offsets,
    radial_weights,
    probe_weight,
    out_weight,
    density_cotangent,
):
    n_slab = lax.axis_size("slab")
    n_dom = lax.axis_size("dom")
    atoms, feature_len = atom_features.shape
    channels = feature_len // COMPONENTS
    slots, probes = probe_atoms.shape
    hslot = halo_lists.shape[2]
    table = n_slab * n_dom * hslot
    quarter = channels // n_dom
    orders = radial_weights.shape[0]
    slab_probes = n_dom * probes
    packed = -(-COMPONENTS // n_dom) * 128
    me = lax.axis_index("dom").astype(jnp.int32).reshape(1)
    groups = -(-COMPONENTS // n_dom)
    wide = pltpu.CompilerParams(vmem_limit_bytes=56 * 2**20)
    narrow = pltpu.CompilerParams(vmem_limit_bytes=(16 if table <= 256 else 56) * 2**20)
    vmem = pl.BlockSpec(memory_space=pltpu.VMEM)
    smem = pl.BlockSpec(memory_space=pltpu.SMEM)
    any_space = pl.BlockSpec(memory_space=pl.ANY)

    send, geometry = pl.pallas_call(
        functools.partial(pack_kernel, n_dom),
        in_specs=[any_space] * 5,
        out_specs=[vmem, vmem],
        out_shape=[
            jax.ShapeDtypeStruct((table, packed), BF),
            jax.ShapeDtypeStruct((5 * slots, probes), F32),
        ],
        scratch_shapes=[
            pltpu.VMEM(atom_features.shape, BF),
            pltpu.VMEM(halo_lists.shape, jnp.int32),
            pltpu.VMEM(offsets.shape, F32),
            pltpu.VMEM(probe_atoms.shape, jnp.int32),
            pltpu.VMEM((1, probes), F32),
            pltpu.SemaphoreType.DMA((4 + groups,)),
        ],
        compiler_params=wide,
        name="pack",
    )(atom_features, halo_lists, offsets, probe_atoms, density_cotangent.reshape(1, probes))
    geo_blocks = spread_over(geometry, n_dom)
    halo = lax.all_to_all(send, ("slab", "dom"), split_axis=0, concat_axis=0, tiled=True)

    y_all, cot, listed, basis, weights = pl.pallas_call(
        functools.partial(basis_kernel, n_dom, channels, slots, probes),
        in_specs=[smem] + [vmem] * (n_dom + 1),
        out_specs=[vmem] * 5,
        scratch_shapes=[
            pltpu.VMEM((5 * slots, slab_probes), F32),
        ],
        out_shape=[
            jax.ShapeDtypeStruct((slots, 32, slab_probes), F32),
            jax.ShapeDtypeStruct((slots, slab_probes), F32),
            jax.ShapeDtypeStruct((slots, slab_probes), jnp.int32),
            jax.ShapeDtypeStruct((3 * orders * slots, slab_probes), BF),
            jax.ShapeDtypeStruct((5 * quarter, 3 * orders * slots), F32),
        ],
        compiler_params=narrow,
        name="basis",
    )(me, *geo_blocks, radial_weights)

    sums, hot, r_all = pl.pallas_call(
        functools.partial(forward_kernel, quarter),
        in_specs=[vmem] * 5,
        out_specs=[vmem] * 3,
        out_shape=[
            jax.ShapeDtypeStruct((quarter, slab_probes), BF),
            jax.ShapeDtypeStruct((slots, table, slab_probes), BF),
            jax.ShapeDtypeStruct((slots, 5 * quarter, slab_probes), F32),
        ],
        scratch_shapes=[
            pltpu.VMEM((packed * n_dom // 128 * quarter, table), BF),
            pltpu.VMEM((quarter, slab_probes), F32),
        ],
        compiler_params=narrow,
        name="forward",
    )(halo, y_all, listed, basis, weights)

    sum_blocks = spread_over(sums, n_dom)

    grads, density = pl.pallas_call(
        functools.partial(backward_kernel, n_dom, quarter, probes),
        in_specs=[smem] + [vmem] * (n_dom + 6),
        out_specs=[vmem, vmem],
        scratch_shapes=[
            pltpu.VMEM((channels, slab_probes), F32),
            pltpu.VMEM((quarter, slab_probes), F32),
            pltpu.VMEM((COMPONENTS * quarter, slab_probes), BF),
            pltpu.VMEM((COMPONENTS * quarter, table), F32),
            pltpu.VMEM((1, slab_probes), F32),
        ],
        out_shape=[
            jax.ShapeDtypeStruct((table, packed), BF),
            jax.ShapeDtypeStruct((1, probes), F32),
        ],
        compiler_params=narrow,
        name="backward",
    )(
        me, *sum_blocks, probe_weight, out_weight.reshape(1, channels), cot, y_all,
        hot, r_all,
    )

    back = lax.all_to_all(grads, ("slab", "dom"), split_axis=0, concat_axis=0, tiled=True)
    atom_grads = pl.pallas_call(
        functools.partial(unpack_kernel, n_dom),
        in_specs=[vmem, vmem],
        out_specs=any_space,
        scratch_shapes=[
            pltpu.VMEM((atoms, feature_len), F32),
            pltpu.SemaphoreType.DMA((groups,)),
        ],
        out_shape=jax.ShapeDtypeStruct((atoms, feature_len), F32),
        compiler_params=narrow,
        name="unpack",
    )(back, halo_lists)
    return (density.reshape(probes), atom_grads)


def solution(mesh):
    return jax.shard_map(
        shards,
        mesh=mesh,
        in_specs=(
            P(("slab", "dom"), None),
            P(None, ("slab", "dom"), None),
            P(None, ("slab", "dom")),
            P(None, None, ("slab", "dom")),
            P(),
            P(),
            P(),
            P(("slab", "dom")),
        ),
        out_specs=(P(("slab", "dom")), P(("slab", "dom"), None)),
        check_vma=False,
    )
```

```python
import functools

import jax
import jax.numpy as jnp
from jax import lax
from jax.experimental import pallas as pl
from jax.experimental.pallas import tpu as pltpu
from jax.sharding import PartitionSpec as P

cutoff_radius = 4.0
COMPONENTS = 25
BF = jnp.bfloat16
F32 = jnp.float32


def iota(shape, dim):
    return lax.broadcasted_iota(jnp.int32, shape, dim)


def dot_nn(a, b):
    return lax.dot_general(a, b, (((1,), (0,)), ((), ())), preferred_element_type=F32)


def dot_nt(a, b):
    return lax.dot_general(a, b, (((1,), (1,)), ((), ())), preferred_element_type=F32)


def dot_tn(a, b):
    return lax.dot_general(a, b, (((0,), (0,)), ((), ())), preferred_element_type=F32)


def split(value):
    high = value.astype(BF)
    return high, (value - high.astype(F32)).astype(BF)


def harmonic_rows(xc, yc, zc):
    xsq = xc * xc
    ysq = yc * yc
    zsq = zc * zc
    return [
        0.28209479 * jnp.ones_like(xc),
        0.48860251 * yc,
        0.48860251 * zc,
        0.48860251 * xc,
        1.09254843 * xc * yc,
        1.09254843 * yc * zc,
        0.31539157 * (3.0 * zsq - 1.0),
        1.09254843 * xc * zc,
        0.54627422 * (xsq - ysq),
        0.59004359 * yc * (3.0 * xsq - ysq),
        2.89061144 * xc * yc * zc,
        0.4570458 * yc * (5.0 * zsq - 1.0),
        0.37317633 * zc * (5.0 * zsq - 3.0),
        0.4570458 * xc * (5.0 * zsq - 1.0),
        1.44530572 * zc * (xsq - ysq),
        0.59004359 * xc * (xsq - 3.0 * ysq),
        2.50334294 * xc * yc * (xsq - ysq),
        1.77013077 * yc * zc * (3.0 * xsq - ysq),
        0.9461747 * xc * yc * (7.0 * zsq - 1.0),
        0.66904654 * yc * zc * (7.0 * zsq - 3.0),
        0.10578555 * (35.0 * zsq * zsq - 30.0 * zsq + 3.0),
        0.66904654 * xc * zc * (7.0 * zsq - 3.0),
        0.47308735 * (xsq - ysq) * (7.0 * zsq - 1.0),
        1.77013077 * xc * zc * (xsq - 3.0 * ysq),
        0.62583574 * (xsq * (xsq - 3.0 * ysq) - ysq * (3.0 * xsq - ysq)),
    ]


def owner_onehot(halo, rows, atoms, hslot):
    n_slab = halo.shape[0]
    pick = (iota((rows, n_slab), 0) // hslot == iota((rows, n_slab), 1)).astype(BF)
    spread = dot_nn(pick, halo.astype(BF))
    mine = iota((rows, hslot), 0) % hslot == iota((rows, hslot), 1)
    column = jnp.sum(jnp.where(mine, spread, 0.0), axis=1, keepdims=True).astype(jnp.int32)
    return (iota((rows, atoms), 1) == column).astype(BF)


def pack_kernel(
    parts,
    h_hbm, halo_hbm, off_hbm, atoms_hbm, cot_hbm,
    out_ref, geo_ref,
    h_ref, halo_ref, off_ref, atoms_ref, cot_ref, sems,
):
    groups = -(-COMPONENTS // parts)
    pairs = [
        (halo_hbm, halo_ref), (h_hbm, h_ref), (off_hbm, off_ref), (atoms_hbm, atoms_ref), (cot_hbm, cot_ref)
    ]
    copies = [
        pltpu.make_async_copy(source, target, sems.at[i]) for i, (source, target) in enumerate(pairs)
    ]
    for copy in copies:
        copy.start()
    copies[0].wait()
    n_slab, hslot = halo_ref.shape[0], halo_ref.shape[2]
    rows = n_slab * hslot
    onehot = owner_onehot(halo_ref[:, 0, :].astype(F32), rows, h_ref.shape[0], hslot)
    for copy in copies[1:]:
        copy.wait()
    slots = atoms_ref.shape[0]
    for i in range(3):
        geo_ref[i * slots : (i + 1) * slots, :] = off_ref[i]
    geo_ref[3 * slots : 4 * slots, :] = atoms_ref[...].astype(F32)
    geo_ref[4 * slots : 5 * slots, :] = jnp.broadcast_to(cot_ref[...], atoms_ref.shape)
    quarter = 128 // parts
    lane_part = iota((rows, 128), 1) // quarter
    for group in range(groups):
        members = min(parts, COMPONENTS - group * parts)
        chosen = dot_nn(onehot, h_ref[:, group * parts * 128 : (group * parts + members) * 128])
        blocks = []
        for part in range(parts):
            total = jnp.zeros((rows, 128), F32)
            for i in range(members):
                source = chosen[:, i * 128 : (i + 1) * 128]
                shift = ((i - part) * quarter) % 128
                if shift:
                    source = pltpu.roll(source, shift, 1)
                total = jnp.where(lane_part == i, source, total)
            blocks.append(total.reshape(n_slab, hslot, 128))
        stacked = jnp.stack(blocks, axis=1).reshape(n_slab * parts * hslot, 128)
        out_ref[:, group * 128 : (group + 1) * 128] = stacked.astype(BF)


def unpack_kernel(parts, hslot, recv_ref, turned_ref, out_hbm, out_ref, sems):
    turned = turned_ref[...]
    rows = turned.shape[1]
    n_slab = rows // hslot
    quarter = 128 // parts
    lane_part = iota((rows, 128), 1) // quarter
    groups = -(-COMPONENTS // parts)
    copies = []
    for group in range(groups):
        members = min(parts, COMPONENTS - group * parts)
        got = recv_ref[:, group * 128 : (group + 1) * 128].astype(F32)
        got = got.reshape(n_slab, parts, hslot, 128)
        pieces = [got[:, part].reshape(rows, 128) for part in range(parts)]
        for i in range(members):
            total = jnp.zeros((rows, 128), F32)
            for part in range(parts):
                shift = ((part - i) * quarter) % 128
                source = pltpu.roll(pieces[part], shift, 1) if shift else pieces[part]
                total = jnp.where(lane_part == part, source, total)
            at = (group * parts + i) * 128
            out_ref[:, at : at + 128] = dot_nn(turned, total.astype(BF))
        lanes = slice(group * parts * 128, (group * parts + members) * 128)
        copy = pltpu.make_async_copy(out_ref.at[:, lanes], out_hbm.at[:, lanes], sems.at[group])
        copy.start()
        copies.append(copy)
    for copy in copies:
        copy.wait()


def basis_kernel(
    parts, orders, slots, probes,
    me_ref, *refs,
):
    blocks = refs[:parts]
    y_all, cot_out, atoms_out, b_all, geo = refs[parts:]
    me = me_ref[0]
    for j in range(parts):
        at = pl.multiple_of((me ^ j) * probes, 128)
        geo[:, pl.ds(at, probes)] = blocks[j][...]
    xo, yo, zo = (geo[i * slots : (i + 1) * slots, :] for i in range(3))
    length = jnp.sqrt(xo * xo + yo * yo + zo * zo)
    angle = jnp.pi * length / cutoff_radius
    sine, cosine = jnp.sin(angle), jnp.cos(angle)
    scale = (2.0 / cutoff_radius) ** 0.5 * (0.5 * (cosine + 1.0)) / length
    before, now = jnp.zeros_like(sine), sine
    high, low = [], []
    for _n in range(orders):
        one, two = split(now * scale)
        high.append(one.astype(F32))
        low.append(two.astype(F32))
        before, now = now, 2.0 * cosine * now - before
    size = orders * slots
    top = jnp.concatenate(high, axis=0).astype(BF)
    b_all[0:size, :] = top
    b_all[size : 2 * size, :] = top
    b_all[2 * size : 3 * size, :] = jnp.concatenate(low, axis=0).astype(BF)
    unit = (xo / length, yo / length, zo / length)
    for index, row in enumerate(harmonic_rows(*unit)):
        row = row.astype(BF).astype(F32)
        for slot in range(slots):
            y_all[slot, index : index + 1, :] = row[slot : slot + 1, :]
    cot_out[...] = geo[4 * slots : 5 * slots, :]
    atoms_out[...] = geo[3 * slots : 4 * slots, :].astype(jnp.int32)


def prepare_kernel(
    parts, channels, slots,
    me_ref, weight_ref, pw_ref, ow_ref, halo_ref, w_all, pw_out, own_out, turned_out,
):
    quarter = channels // parts
    orders = weight_ref.shape[0]
    me = me_ref[0]
    weights = weight_ref[...]
    w_high, w_low = split(weights)
    w_high, w_low = w_high.astype(F32), w_low.astype(F32)
    spread = []
    for source in (w_high, w_low, w_high):
        for n in range(orders):
            spread.append(jnp.broadcast_to(source[n : n + 1, :], (slots, 5 * channels)))
    spread = jnp.concatenate(spread, axis=0).astype(BF)
    row = iota((5 * quarter, 5 * channels), 0)
    wanted = row // quarter * channels + me * quarter + row % quarter
    choose = (iota((5 * quarter, 5 * channels), 1) == wanted).astype(BF)
    w_all[...] = dot_nt(choose, spread)
    p_high, p_low = split(pw_ref[...].T)
    pw_out[:, 0:channels] = p_high
    pw_out[:, channels : 2 * channels] = p_low
    own = pw_ref[pl.ds(pl.multiple_of(me * quarter, quarter), quarter), :]
    eye = iota((channels, channels), 0) == iota((channels, channels), 1)
    column = jnp.sum(jnp.where(eye, ow_ref[...], 0.0), axis=1, keepdims=True)
    own_out[0:quarter, :] = own
    own_out[quarter : quarter + channels, :] = jnp.broadcast_to(column, (channels, channels))
    n_slab, hslot = halo_ref.shape[0], halo_ref.shape[2]
    onehot = owner_onehot(halo_ref[:, 0, :].astype(F32), n_slab * hslot, turned_out.shape[0], hslot)
    turned_out[...] = onehot.astype(F32).T.astype(BF)


def radial(k, slots, w_ref, b_ref, lanes):
    weights = w_ref[...]
    mine = jnp.where(iota(weights.shape, 1) % slots == k, weights, 0.0).astype(BF)
    return dot_nn(mine, b_ref[:, lanes])


def onehot_of(k, atoms_ref, table, lanes):
    atoms = atoms_ref[k : k + 1, lanes]
    return (iota((table, atoms.shape[1]), 0) == atoms).astype(F32).astype(BF)


def forward_kernel(
    quarter, h_ref, y_ref, atoms_ref, b_ref, w_ref, s_ref, hot_ref, r_ref, turned, total
):
    slots, table = atoms_ref.shape[0], h_ref.shape[0]
    turned[...] = h_ref[...].astype(F32).T.astype(BF)
    total[...] = jnp.zeros_like(total)
    width = total.shape[1]
    step = 256

    for k in range(slots):
        for at in range(0, width, step):
            lanes = slice(at, at + step)
            hot = onehot_of(k, atoms_ref, table, lanes)
            rad = radial(k, slots, w_ref, b_ref, lanes)
            hot_ref[k, :, lanes] = hot
            r_ref[k, :, lanes] = rad
            got = dot_nn(turned[0 : COMPONENTS * quarter, :], hot)
            acc = total[:, lanes]
            for degree in range(5):
                first, last = degree * degree, (degree + 1) ** 2
                inner = got[first * quarter : (first + 1) * quarter] * y_ref[k, first : first + 1, lanes]
                for m in range(first + 1, last):
                    inner = inner + (
                        got[m * quarter : (m + 1) * quarter] * y_ref[k, m : m + 1, lanes]
                    )
                acc = acc + inner * rad[degree * quarter : (degree + 1) * quarter]
            total[:, lanes] = acc
    s_ref[...] = total[...].astype(BF)


def backward_kernel(
    parts, quarter, probes,
    me_ref, *refs,
):
    sums = refs[:parts]
    pw_ref, own_ref, cot_ref, y_ref, hot_ref, r_ref = refs[parts : parts + 6]
    grads_ref, density_ref, s_all, ds, z, acc, dens = refs[parts + 6 :]
    slots = y_ref.shape[0]
    me = me_ref[0]
    channels = parts * quarter
    for j in range(parts):
        at = pl.multiple_of((me ^ j) * quarter, quarter)
        s_all[pl.ds(at, quarter), :] = sums[j][...].astype(F32)
    given = s_all[...].astype(BF)
    pre = dot_nn(pw_ref[:, 0:channels], given) + dot_nn(pw_ref[:, channels : 2 * channels], given)
    ow = own_ref[quarter : quarter + channels, 0:1]
    sigma = 1.0 / (1.0 + jnp.exp(-pre))
    dens[...] = jnp.sum(pre * sigma * ow, axis=0, keepdims=True)
    here = pl.multiple_of(me * probes, 128)
    density_ref[...] = dens[:, pl.ds(here, probes)]
    dpre = cot_ref[0:1, :] * ow * sigma * (1.0 + pre * (1.0 - sigma))
    d_high, d_low = split(dpre)
    o_high, o_low = split(own_ref[0:quarter, :])
    ds[...] = dot_nn(o_high, d_high) + dot_nn(o_high, d_low) + dot_nn(o_low, d_high)
    acc[...] = jnp.zeros_like(acc)

    for k in range(slots):
        for degree in range(5):
            first, last = degree * degree, (degree + 1) ** 2
            weighted = ds[...] * r_ref[k, degree * quarter : (degree + 1) * quarter, :]
            for m in range(first, last):
                z[m * quarter : (m + 1) * quarter, :] = (
                    weighted * y_ref[k, m : m + 1, :]
                ).astype(BF)
        acc[...] += dot_nt(z[...], hot_ref[k])

    filled = (COMPONENTS * quarter) // 128 * 128
    grads_ref[:, 0:filled] = acc[0:filled, :].T.astype(BF)
    rest = acc[filled : COMPONENTS * quarter, :]
    space = grads_ref.shape[1] - COMPONENTS * quarter
    rest = jnp.concatenate([rest, jnp.zeros((space, rest.shape[1]), F32)], axis=0)
    grads_ref[:, filled:] = rest.T.astype(BF)


def spread_over(value, n_dom):
    blocks = {0: value}
    bit = n_dom // 2
    while bit:
        pairs = [(i, i ^ bit) for i in range(n_dom)]
        for j in list(blocks):
            blocks[j | bit] = lax.ppermute(blocks[j], "dom", pairs)
        bit //= 2
    return [blocks[j] for j in range(n_dom)]


def shards(
    atom_features,
    halo_lists,
    probe_atoms,
    offsets,
    radial_weights,
    probe_weight,
    out_weight,
    density_cotangent,
):
    n_slab = lax.axis_size("slab")
    n_dom = lax.axis_size("dom")
    atoms, feature_len = atom_features.shape
    channels = feature_len // COMPONENTS
    slots, probes = probe_atoms.shape
    hslot = halo_lists.shape[2]
    table = n_slab * n_dom * hslot
    quarter = channels // n_dom
    orders = radial_weights.shape[0]
    slab_probes = n_dom * probes
    packed = -(-COMPONENTS // n_dom) * 128
    me = lax.axis_index("dom").astype(jnp.int32).reshape(1)
    groups = -(-COMPONENTS // n_dom)
    wide = pltpu.CompilerParams(vmem_limit_bytes=56 * 2**20)
    narrow = pltpu.CompilerParams(vmem_limit_bytes=(16 if table <= 256 else 56) * 2**20)
    vmem = pl.BlockSpec(memory_space=pltpu.VMEM)
    smem = pl.BlockSpec(memory_space=pltpu.SMEM)
    any_space = pl.BlockSpec(memory_space=pl.ANY)

    send, geometry = pl.pallas_call(
        functools.partial(pack_kernel, n_dom),
        in_specs=[any_space] * 5,
        out_specs=[vmem, vmem],
        out_shape=[
            jax.ShapeDtypeStruct((table, packed), BF),
            jax.ShapeDtypeStruct((5 * slots, probes), F32),
        ],
        scratch_shapes=[
            pltpu.VMEM(atom_features.shape, BF),
            pltpu.VMEM(halo_lists.shape, jnp.int32),
            pltpu.VMEM(offsets.shape, F32),
            pltpu.VMEM(probe_atoms.shape, jnp.int32),
            pltpu.VMEM((1, probes), F32),
            pltpu.SemaphoreType.DMA((5,)),
        ],
        compiler_params=wide,
        name="pack",
    )(atom_features, halo_lists, offsets, probe_atoms, density_cotangent.reshape(1, probes))
    geo_blocks = spread_over(geometry, n_dom)
    halo = lax.all_to_all(send, ("slab", "dom"), split_axis=0, concat_axis=0, tiled=True)

    weights, mixing, readout, turned = pl.pallas_call(
        functools.partial(prepare_kernel, n_dom, channels, slots),
        in_specs=[smem] + [vmem] * 4,
        out_specs=[vmem] * 4,
        out_shape=[
            jax.ShapeDtypeStruct((5 * quarter, 3 * orders * slots), F32),
            jax.ShapeDtypeStruct((channels, 2 * channels), BF),
            jax.ShapeDtypeStruct((quarter + channels, channels), F32),
            jax.ShapeDtypeStruct((atoms, n_slab * hslot), BF),
        ],
        compiler_params=narrow,
        name="prepare",
    )(me, radial_weights, probe_weight, out_weight.reshape(1, channels), halo_lists)

    y_all, cot, listed, basis = pl.pallas_call(
        functools.partial(basis_kernel, n_dom, orders, slots, probes),
        in_specs=[smem] + [vmem] * n_dom,
        out_specs=[vmem] * 4,
        scratch_shapes=[pltpu.VMEM((5 * slots, slab_probes), F32)],
        out_shape=[
            jax.ShapeDtypeStruct((slots, 32, slab_probes), F32),
            jax.ShapeDtypeStruct((slots, slab_probes), F32),
            jax.ShapeDtypeStruct((slots, slab_probes), jnp.int32),
            jax.ShapeDtypeStruct((3 * orders * slots, slab_probes), BF),
        ],
        compiler_params=narrow,
        name="basis",
    )(me, *geo_blocks)

    sums, hot, r_all = pl.pallas_call(
        functools.partial(forward_kernel, quarter),
        in_specs=[vmem] * 5,
        out_specs=[vmem] * 3,
        out_shape=[
            jax.ShapeDtypeStruct((quarter, slab_probes), BF),
            jax.ShapeDtypeStruct((slots, table, slab_probes), BF),
            jax.ShapeDtypeStruct((slots, 5 * quarter, slab_probes), F32),
        ],
        scratch_shapes=[
            pltpu.VMEM((packed * n_dom // 128 * quarter, table), BF),
            pltpu.VMEM((quarter, slab_probes), F32),
        ],
        compiler_params=narrow,
        name="forward",
    )(halo, y_all, listed, basis, weights)

    sum_blocks = spread_over(sums, n_dom)

    grads, density = pl.pallas_call(
        functools.partial(backward_kernel, n_dom, quarter, probes),
        in_specs=[smem] + [vmem] * (n_dom + 6),
        out_specs=[vmem, vmem],
        scratch_shapes=[
            pltpu.VMEM((channels, slab_probes), F32),
            pltpu.VMEM((quarter, slab_probes), F32),
            pltpu.VMEM((COMPONENTS * quarter, slab_probes), BF),
            pltpu.VMEM((COMPONENTS * quarter, table), F32),
            pltpu.VMEM((1, slab_probes), F32),
        ],
        out_shape=[
            jax.ShapeDtypeStruct((table, packed), BF),
            jax.ShapeDtypeStruct((1, probes), F32),
        ],
        compiler_params=narrow,
        name="backward",
    )(
        me, *sum_blocks, mixing, readout, cot, y_all,
        hot, r_all,
    )

    back = lax.all_to_all(grads, ("slab", "dom"), split_axis=0, concat_axis=0, tiled=True)
    atom_grads = pl.pallas_call(
        functools.partial(unpack_kernel, n_dom, hslot),
        in_specs=[vmem, vmem],
        out_specs=any_space,
        scratch_shapes=[
            pltpu.VMEM((atoms, feature_len), F32),
            pltpu.SemaphoreType.DMA((groups,)),
        ],
        out_shape=jax.ShapeDtypeStruct((atoms, feature_len), F32),
        compiler_params=narrow,
        name="unpack",
    )(back, turned)
    return (density.reshape(probes), atom_grads)


def solution(mesh):
    return jax.shard_map(
        shards,
        mesh=mesh,
        in_specs=(
            P(("slab", "dom"), None),
            P(None, ("slab", "dom"), None),
            P(None, ("slab", "dom")),
            P(None, None, ("slab", "dom")),
            P(),
            P(),
            P(),
            P(("slab", "dom")),
        ),
        out_specs=(P(("slab", "dom")), P(("slab", "dom"), None)),
        check_vma=False,
    )
```

```python
import functools

import jax
import jax.numpy as jnp
from jax import lax
from jax.experimental import pallas as pl
from jax.experimental.pallas import tpu as pltpu
from jax.sharding import PartitionSpec as P

cutoff_radius = 4.0
COMPONENTS = 25
BF = jnp.bfloat16
F32 = jnp.float32


def iota(shape, dim):
    return lax.broadcasted_iota(jnp.int32, shape, dim)


def dot_nn(a, b):
    return lax.dot_general(a, b, (((1,), (0,)), ((), ())), preferred_element_type=F32)


def dot_nt(a, b):
    return lax.dot_general(a, b, (((1,), (1,)), ((), ())), preferred_element_type=F32)


def dot_tn(a, b):
    return lax.dot_general(a, b, (((0,), (0,)), ((), ())), preferred_element_type=F32)


def split(value):
    high = value.astype(BF)
    return high, (value - high.astype(F32)).astype(BF)


def harmonic_rows(xc, yc, zc):
    xsq = xc * xc
    ysq = yc * yc
    zsq = zc * zc
    return [
        0.28209479 * jnp.ones_like(xc),
        0.48860251 * yc,
        0.48860251 * zc,
        0.48860251 * xc,
        1.09254843 * xc * yc,
        1.09254843 * yc * zc,
        0.31539157 * (3.0 * zsq - 1.0),
        1.09254843 * xc * zc,
        0.54627422 * (xsq - ysq),
        0.59004359 * yc * (3.0 * xsq - ysq),
        2.89061144 * xc * yc * zc,
        0.4570458 * yc * (5.0 * zsq - 1.0),
        0.37317633 * zc * (5.0 * zsq - 3.0),
        0.4570458 * xc * (5.0 * zsq - 1.0),
        1.44530572 * zc * (xsq - ysq),
        0.59004359 * xc * (xsq - 3.0 * ysq),
        2.50334294 * xc * yc * (xsq - ysq),
        1.77013077 * yc * zc * (3.0 * xsq - ysq),
        0.9461747 * xc * yc * (7.0 * zsq - 1.0),
        0.66904654 * yc * zc * (7.0 * zsq - 3.0),
        0.10578555 * (35.0 * zsq * zsq - 30.0 * zsq + 3.0),
        0.66904654 * xc * zc * (7.0 * zsq - 3.0),
        0.47308735 * (xsq - ysq) * (7.0 * zsq - 1.0),
        1.77013077 * xc * zc * (xsq - 3.0 * ysq),
        0.62583574 * (xsq * (xsq - 3.0 * ysq) - ysq * (3.0 * xsq - ysq)),
    ]


def owner_onehot(halo, rows, atoms, hslot):
    n_slab = halo.shape[0]
    pick = (iota((rows, n_slab), 0) // hslot == iota((rows, n_slab), 1)).astype(BF)
    spread = dot_nn(pick, halo.astype(BF))
    mine = iota((rows, hslot), 0) % hslot == iota((rows, hslot), 1)
    column = jnp.sum(jnp.where(mine, spread, 0.0), axis=1, keepdims=True).astype(jnp.int32)
    return (iota((rows, atoms), 1) == column).astype(BF)


def pack_kernel(
    parts,
    h_hbm, halo_hbm, off_hbm, atoms_hbm, cot_hbm,
    out_ref, geo_ref,
    h_ref, halo_ref, off_ref, atoms_ref, cot_ref, sems,
):
    groups = -(-COMPONENTS // parts)
    pairs = [
        (halo_hbm, halo_ref), (h_hbm, h_ref), (off_hbm, off_ref), (atoms_hbm, atoms_ref), (cot_hbm, cot_ref)
    ]
    copies = [
        pltpu.make_async_copy(source, target, sems.at[i]) for i, (source, target) in enumerate(pairs)
    ]
    for copy in copies:
        copy.start()
    copies[0].wait()
    n_slab, hslot = halo_ref.shape[0], halo_ref.shape[2]
    rows = n_slab * hslot
    onehot = owner_onehot(halo_ref[:, 0, :].astype(F32), rows, h_ref.shape[0], hslot)
    for copy in copies[1:]:
        copy.wait()
    slots = atoms_ref.shape[0]
    for i in range(3):
        geo_ref[i * slots : (i + 1) * slots, :] = off_ref[i]
    geo_ref[3 * slots : 4 * slots, :] = atoms_ref[...].astype(F32)
    geo_ref[4 * slots : 5 * slots, :] = jnp.broadcast_to(cot_ref[...], atoms_ref.shape)
    quarter = 128 // parts
    lane_part = iota((rows, 128), 1) // quarter
    for group in range(groups):
        members = min(parts, COMPONENTS - group * parts)
        chosen = dot_nn(onehot, h_ref[:, group * parts * 128 : (group * parts + members) * 128])
        blocks = []
        for part in range(parts):
            total = jnp.zeros((rows, 128), F32)
            for i in range(members):
                source = chosen[:, i * 128 : (i + 1) * 128]
                shift = ((i - part) * quarter) % 128
                if shift:
                    source = pltpu.roll(source, shift, 1)
                total = jnp.where(lane_part == i, source, total)
            blocks.append(total.reshape(n_slab, hslot, 128))
        stacked = jnp.stack(blocks, axis=1).reshape(n_slab * parts * hslot, 128)
        out_ref[:, group * 128 : (group + 1) * 128] = stacked.astype(BF)


def unpack_kernel(parts, hslot, recv_ref, turned_ref, out_hbm, out_ref, sems):
    turned = turned_ref[...]
    rows = turned.shape[1]
    n_slab = rows // hslot
    quarter = 128 // parts
    lane_part = iota((rows, 128), 1) // quarter
    groups = -(-COMPONENTS // parts)
    copies = []
    for group in range(groups):
        members = min(parts, COMPONENTS - group * parts)
        got = recv_ref[:, group * 128 : (group + 1) * 128].astype(F32)
        got = got.reshape(n_slab, parts, hslot, 128)
        pieces = [got[:, part].reshape(rows, 128) for part in range(parts)]
        for i in range(members):
            total = jnp.zeros((rows, 128), F32)
            for part in range(parts):
                shift = ((part - i) * quarter) % 128
                source = pltpu.roll(pieces[part], shift, 1) if shift else pieces[part]
                total = jnp.where(lane_part == part, source, total)
            at = (group * parts + i) * 128
            out_ref[:, at : at + 128] = dot_nn(turned, total.astype(BF))
        lanes = slice(group * parts * 128, (group * parts + members) * 128)
        copy = pltpu.make_async_copy(out_ref.at[:, lanes], out_hbm.at[:, lanes], sems.at[group])
        copy.start()
        copies.append(copy)
    for copy in copies:
        copy.wait()


def basis_kernel(
    parts, orders, slots, probes,
    me_ref, *refs,
):
    blocks = refs[:parts]
    y_all, cot_out, atoms_out, b_all, geo = refs[parts:]
    me = me_ref[0]
    for j in range(parts):
        at = pl.multiple_of((me ^ j) * probes, 128)
        geo[:, pl.ds(at, probes)] = blocks[j][...]
    xo, yo, zo = (geo[i * slots : (i + 1) * slots, :] for i in range(3))
    length = jnp.sqrt(xo * xo + yo * yo + zo * zo)
    angle = jnp.pi * length / cutoff_radius
    sine, cosine = jnp.sin(angle), jnp.cos(angle)
    scale = (2.0 / cutoff_radius) ** 0.5 * (0.5 * (cosine + 1.0)) / length
    before, now = jnp.zeros_like(sine), sine
    high, low = [], []
    for _n in range(orders):
        one, two = split(now * scale)
        high.append(one.astype(F32))
        low.append(two.astype(F32))
        before, now = now, 2.0 * cosine * now - before
    size = orders * slots
    top = jnp.concatenate(high, axis=0).astype(BF)
    b_all[0:size, :] = top
    b_all[size : 2 * size, :] = top
    b_all[2 * size : 3 * size, :] = jnp.concatenate(low, axis=0).astype(BF)
    unit = (xo / length, yo / length, zo / length)
    for index, row in enumerate(harmonic_rows(*unit)):
        row = row.astype(BF).astype(F32)
        for slot in range(slots):
            y_all[slot, index : index + 1, :] = row[slot : slot + 1, :]
    cot_out[...] = geo[4 * slots : 5 * slots, :]
    atoms_out[...] = geo[3 * slots : 4 * slots, :].astype(jnp.int32)


def prepare_kernel(
    parts, channels, slots,
    me_ref, weight_ref, pw_ref, ow_ref, halo_ref, w_all, pw_out, own_out, turned_out,
):
    quarter = channels // parts
    orders = weight_ref.shape[0]
    me = me_ref[0]
    weights = weight_ref[...]
    w_high, w_low = split(weights)
    w_high, w_low = w_high.astype(F32), w_low.astype(F32)
    spread = []
    for source in (w_high, w_low, w_high):
        for n in range(orders):
            spread.append(jnp.broadcast_to(source[n : n + 1, :], (slots, 5 * channels)))
    spread = jnp.concatenate(spread, axis=0).astype(BF)
    row = iota((5 * quarter, 5 * channels), 0)
    wanted = row // quarter * channels + me * quarter + row % quarter
    choose = (iota((5 * quarter, 5 * channels), 1) == wanted).astype(BF)
    w_all[...] = dot_nt(choose, spread)
    p_high, p_low = split(pw_ref[...].T)
    pw_out[:, 0:channels] = p_high
    pw_out[:, channels : 2 * channels] = p_low
    own = pw_ref[pl.ds(pl.multiple_of(me * quarter, quarter), quarter), :]
    eye = iota((channels, channels), 0) == iota((channels, channels), 1)
    column = jnp.sum(jnp.where(eye, ow_ref[...], 0.0), axis=1, keepdims=True)
    own_out[0:quarter, :] = own
    own_out[quarter : quarter + channels, :] = jnp.broadcast_to(column, (channels, channels))
    n_slab, hslot = halo_ref.shape[0], halo_ref.shape[2]
    onehot = owner_onehot(halo_ref[:, 0, :].astype(F32), n_slab * hslot, turned_out.shape[0], hslot)
    turned_out[...] = onehot.astype(F32).T.astype(BF)


def radial(k, slots, w_ref, b_ref, lanes):
    weights = w_ref[...]
    mine = jnp.where(iota(weights.shape, 1) % slots == k, weights, 0.0).astype(BF)
    return dot_nn(mine, b_ref[:, lanes])


def onehot_of(k, atoms_ref, table, lanes):
    atoms = atoms_ref[k : k + 1, lanes]
    return (iota((table, atoms.shape[1]), 0) == atoms).astype(F32).astype(BF)


def forward_kernel(
    quarter, h_ref, y_ref, atoms_ref, b_ref, w_ref, s_ref, hot_ref, r_ref, turned, total
):
    slots, table = atoms_ref.shape[0], h_ref.shape[0]
    turned[...] = h_ref[...].astype(F32).T.astype(BF)
    total[...] = jnp.zeros_like(total)
    for k in range(slots):
        hot = onehot_of(k, atoms_ref, table, slice(None))
        rad = radial(k, slots, w_ref, b_ref, slice(None))
        hot_ref[k] = hot
        r_ref[k] = rad
        got = dot_nn(turned[0 : COMPONENTS * quarter, :], hot)
        acc = total[...]
        for degree in range(5):
            first, last = degree * degree, (degree + 1) ** 2
            inner = got[first * quarter : (first + 1) * quarter] * y_ref[k, first : first + 1, :]
            for m in range(first + 1, last):
                inner = inner + got[m * quarter : (m + 1) * quarter] * y_ref[k, m : m + 1, :]
            acc = acc + inner * rad[degree * quarter : (degree + 1) * quarter]
        total[...] = acc

    s_ref[...] = total[...].astype(BF)


def backward_kernel(
    parts, quarter, probes,
    me_ref, *refs,
):
    sums = refs[:parts]
    pw_ref, own_ref, cot_ref, y_ref, hot_ref, r_ref = refs[parts : parts + 6]
    grads_ref, density_ref, s_all, ds, z, acc, dens = refs[parts + 6 :]
    slots = y_ref.shape[0]
    me = me_ref[0]
    channels = parts * quarter
    for j in range(parts):
        at = pl.multiple_of((me ^ j) * quarter, quarter)
        s_all[pl.ds(at, quarter), :] = sums[j][...].astype(F32)
    given = s_all[...].astype(BF)
    pre = dot_nn(pw_ref[:, 0:channels], given) + dot_nn(pw_ref[:, channels : 2 * channels], given)
    ow = own_ref[quarter : quarter + channels, 0:1]
    sigma = 1.0 / (1.0 + jnp.exp(-pre))
    dens[...] = jnp.sum(pre * sigma * ow, axis=0, keepdims=True)
    here = pl.multiple_of(me * probes, 128)
    density_ref[...] = dens[:, pl.ds(here, probes)]
    dpre = cot_ref[0:1, :] * ow * sigma * (1.0 + pre * (1.0 - sigma))
    d_high, d_low = split(dpre)
    o_high, o_low = split(own_ref[0:quarter, :])
    ds[...] = dot_nn(o_high, d_high) + dot_nn(o_high, d_low) + dot_nn(o_low, d_high)
    acc[...] = jnp.zeros_like(acc)

    for k in range(slots):
        for degree in range(5):
            first, last = degree * degree, (degree + 1) ** 2
            weighted = ds[...] * r_ref[k, degree * quarter : (degree + 1) * quarter, :]
            for m in range(first, last):
                z[m * quarter : (m + 1) * quarter, :] = (
                    weighted * y_ref[k, m : m + 1, :]
                ).astype(BF)
        acc[...] += dot_nt(z[...], hot_ref[k])

    filled = (COMPONENTS * quarter) // 128 * 128
    grads_ref[:, 0:filled] = acc[0:filled, :].T.astype(BF)
    rest = acc[filled : COMPONENTS * quarter, :]
    space = grads_ref.shape[1] - COMPONENTS * quarter
    rest = jnp.concatenate([rest, jnp.zeros((space, rest.shape[1]), F32)], axis=0)
    grads_ref[:, filled:] = rest.T.astype(BF)


def spread_over(value, n_dom):
    blocks = {0: value}
    bit = n_dom // 2
    while bit:
        pairs = [(i, i ^ bit) for i in range(n_dom)]
        for j in list(blocks):
            blocks[j | bit] = lax.ppermute(blocks[j], "dom", pairs)
        bit //= 2
    return [blocks[j] for j in range(n_dom)]


def shards(
    atom_features,
    halo_lists,
    probe_atoms,
    offsets,
    radial_weights,
    probe_weight,
    out_weight,
    density_cotangent,
):
    n_slab = lax.axis_size("slab")
    n_dom = lax.axis_size("dom")
    atoms, feature_len = atom_features.shape
    channels = feature_len // COMPONENTS
    slots, probes = probe_atoms.shape
    hslot = halo_lists.shape[2]
    table = n_slab * n_dom * hslot
    quarter = channels // n_dom
    orders = radial_weights.shape[0]
    slab_probes = n_dom * probes
    packed = -(-COMPONENTS // n_dom) * 128
    me = lax.axis_index("dom").astype(jnp.int32).reshape(1)
    groups = -(-COMPONENTS // n_dom)
    wide = pltpu.CompilerParams(vmem_limit_bytes=56 * 2**20)
    narrow = pltpu.CompilerParams(vmem_limit_bytes=(16 if table <= 256 else 56) * 2**20)
    vmem = pl.BlockSpec(memory_space=pltpu.VMEM)
    smem = pl.BlockSpec(memory_space=pltpu.SMEM)
    any_space = pl.BlockSpec(memory_space=pl.ANY)

    send, geometry = pl.pallas_call(
        functools.partial(pack_kernel, n_dom),
        in_specs=[any_space] * 5,
        out_specs=[vmem, vmem],
        out_shape=[
            jax.ShapeDtypeStruct((table, packed), BF),
            jax.ShapeDtypeStruct((5 * slots, probes), F32),
        ],
        scratch_shapes=[
            pltpu.VMEM(atom_features.shape, BF),
            pltpu.VMEM(halo_lists.shape, jnp.int32),
            pltpu.VMEM(offsets.shape, F32),
            pltpu.VMEM(probe_atoms.shape, jnp.int32),
            pltpu.VMEM((1, probes), F32),
            pltpu.SemaphoreType.DMA((5,)),
        ],
        compiler_params=wide,
        name="pack",
    )(atom_features, halo_lists, offsets, probe_atoms, density_cotangent.reshape(1, probes))
    geo_blocks = spread_over(geometry, n_dom)
    halo = lax.all_to_all(send, ("slab", "dom"), split_axis=0, concat_axis=0, tiled=True)

    weights, mixing, readout, turned = pl.pallas_call(
        functools.partial(prepare_kernel, n_dom, channels, slots),
        in_specs=[smem] + [vmem] * 4,
        out_specs=[vmem] * 4,
        out_shape=[
            jax.ShapeDtypeStruct((5 * quarter, 3 * orders * slots), F32),
            jax.ShapeDtypeStruct((channels, 2 * channels), BF),
            jax.ShapeDtypeStruct((quarter + channels, channels), F32),
            jax.ShapeDtypeStruct((atoms, n_slab * hslot), BF),
        ],
        compiler_params=narrow,
        name="prepare",
    )(me, radial_weights, probe_weight, out_weight.reshape(1, channels), halo_lists)

    y_all, cot, listed, basis = pl.pallas_call(
        functools.partial(basis_kernel, n_dom, orders, slots, probes),
        in_specs=[smem] + [vmem] * n_dom,
        out_specs=[vmem] * 4,
        scratch_shapes=[pltpu.VMEM((5 * slots, slab_probes), F32)],
        out_shape=[
            jax.ShapeDtypeStruct((slots, 32, slab_probes), F32),
            jax.ShapeDtypeStruct((slots, slab_probes), F32),
            jax.ShapeDtypeStruct((slots, slab_probes), jnp.int32),
            jax.ShapeDtypeStruct((3 * orders * slots, slab_probes), BF),
        ],
        compiler_params=narrow,
        name="basis",
    )(me, *geo_blocks)

    sums, hot, r_all = pl.pallas_call(
        functools.partial(forward_kernel, quarter),
        in_specs=[vmem] * 5,
        out_specs=[vmem] * 3,
        out_shape=[
            jax.ShapeDtypeStruct((quarter, slab_probes), BF),
            jax.ShapeDtypeStruct((slots, table, slab_probes), BF),
            jax.ShapeDtypeStruct((slots, 5 * quarter, slab_probes), F32),
        ],
        scratch_shapes=[
            pltpu.VMEM((packed * n_dom // 128 * quarter, table), BF),
            pltpu.VMEM((quarter, slab_probes), F32),
        ],
        compiler_params=narrow,
        name="forward",
    )(halo, y_all, listed, basis, weights)

    sum_blocks = spread_over(sums, n_dom)

    grads, density = pl.pallas_call(
        functools.partial(backward_kernel, n_dom, quarter, probes),
        in_specs=[smem] + [vmem] * (n_dom + 6),
        out_specs=[vmem, vmem],
        scratch_shapes=[
            pltpu.VMEM((channels, slab_probes), F32),
            pltpu.VMEM((quarter, slab_probes), F32),
            pltpu.VMEM((COMPONENTS * quarter, slab_probes), BF),
            pltpu.VMEM((COMPONENTS * quarter, table), F32),
            pltpu.VMEM((1, slab_probes), F32),
        ],
        out_shape=[
            jax.ShapeDtypeStruct((table, packed), BF),
            jax.ShapeDtypeStruct((1, probes), F32),
        ],
        compiler_params=narrow,
        name="backward",
    )(
        me, *sum_blocks, mixing, readout, cot, y_all,
        hot, r_all,
    )

    back = lax.all_to_all(grads, ("slab", "dom"), split_axis=0, concat_axis=0, tiled=True)
    atom_grads = pl.pallas_call(
        functools.partial(unpack_kernel, n_dom, hslot),
        in_specs=[vmem, vmem],
        out_specs=any_space,
        scratch_shapes=[
            pltpu.VMEM((atoms, feature_len), F32),
            pltpu.SemaphoreType.DMA((groups,)),
        ],
        out_shape=jax.ShapeDtypeStruct((atoms, feature_len), F32),
        compiler_params=narrow,
        name="unpack",
    )(back, turned)
    return (density.reshape(probes), atom_grads)


def solution(mesh):
    return jax.shard_map(
        shards,
        mesh=mesh,
        in_specs=(
            P(("slab", "dom"), None),
            P(None, ("slab", "dom"), None),
            P(None, ("slab", "dom")),
            P(None, None, ("slab", "dom")),
            P(),
            P(),
            P(),
            P(("slab", "dom")),
        ),
        out_specs=(P(("slab", "dom")), P(("slab", "dom"), None)),
        check_vma=False,
    )
```

```python
import functools

import jax
import jax.numpy as jnp
from jax import lax
from jax.experimental import pallas as pl
from jax.experimental.pallas import tpu as pltpu
from jax.sharding import PartitionSpec as P

cutoff_radius = 4.0
COMPONENTS = 25
BF = jnp.bfloat16
F32 = jnp.float32


def iota(shape, dim):
    return lax.broadcasted_iota(jnp.int32, shape, dim)


def dot_nn(a, b):
    return lax.dot_general(a, b, (((1,), (0,)), ((), ())), preferred_element_type=F32)


def dot_nt(a, b):
    return lax.dot_general(a, b, (((1,), (1,)), ((), ())), preferred_element_type=F32)


def dot_tn(a, b):
    return lax.dot_general(a, b, (((0,), (0,)), ((), ())), preferred_element_type=F32)


def split(value):
    high = value.astype(BF)
    return high, (value - high.astype(F32)).astype(BF)


def harmonic_rows(xc, yc, zc):
    xsq = xc * xc
    ysq = yc * yc
    zsq = zc * zc
    return [
        0.28209479 * jnp.ones_like(xc),
        0.48860251 * yc,
        0.48860251 * zc,
        0.48860251 * xc,
        1.09254843 * xc * yc,
        1.09254843 * yc * zc,
        0.31539157 * (3.0 * zsq - 1.0),
        1.09254843 * xc * zc,
        0.54627422 * (xsq - ysq),
        0.59004359 * yc * (3.0 * xsq - ysq),
        2.89061144 * xc * yc * zc,
        0.4570458 * yc * (5.0 * zsq - 1.0),
        0.37317633 * zc * (5.0 * zsq - 3.0),
        0.4570458 * xc * (5.0 * zsq - 1.0),
        1.44530572 * zc * (xsq - ysq),
        0.59004359 * xc * (xsq - 3.0 * ysq),
        2.50334294 * xc * yc * (xsq - ysq),
        1.77013077 * yc * zc * (3.0 * xsq - ysq),
        0.9461747 * xc * yc * (7.0 * zsq - 1.0),
        0.66904654 * yc * zc * (7.0 * zsq - 3.0),
        0.10578555 * (35.0 * zsq * zsq - 30.0 * zsq + 3.0),
        0.66904654 * xc * zc * (7.0 * zsq - 3.0),
        0.47308735 * (xsq - ysq) * (7.0 * zsq - 1.0),
        1.77013077 * xc * zc * (xsq - 3.0 * ysq),
        0.62583574 * (xsq * (xsq - 3.0 * ysq) - ysq * (3.0 * xsq - ysq)),
    ]


def owner_onehot(halo, rows, atoms, hslot):
    n_slab = halo.shape[0]
    pick = (iota((rows, n_slab), 0) // hslot == iota((rows, n_slab), 1)).astype(BF)
    spread = dot_nn(pick, halo.astype(BF))
    mine = iota((rows, hslot), 0) % hslot == iota((rows, hslot), 1)
    column = jnp.sum(jnp.where(mine, spread, 0.0), axis=1, keepdims=True).astype(jnp.int32)
    return (iota((rows, atoms), 1) == column).astype(BF)


def pack_kernel(
    parts,
    h_hbm, halo_hbm, off_hbm, atoms_hbm, cot_hbm,
    out_ref, geo_ref,
    h_ref, halo_ref, off_ref, atoms_ref, cot_ref, sems,
):
    groups = -(-COMPONENTS // parts)
    pairs = [
        (halo_hbm, halo_ref), (h_hbm, h_ref), (off_hbm, off_ref), (atoms_hbm, atoms_ref), (cot_hbm, cot_ref)
    ]
    copies = [
        pltpu.make_async_copy(source, target, sems.at[i]) for i, (source, target) in enumerate(pairs)
    ]
    for copy in copies:
        copy.start()
    copies[0].wait()
    n_slab, hslot = halo_ref.shape[0], halo_ref.shape[2]
    rows = n_slab * hslot
    onehot = owner_onehot(halo_ref[:, 0, :].astype(F32), rows, h_ref.shape[0], hslot)
    for copy in copies[1:]:
        copy.wait()
    slots = atoms_ref.shape[0]
    for i in range(3):
        geo_ref[i * slots : (i + 1) * slots, :] = off_ref[i]
    geo_ref[3 * slots : 4 * slots, :] = atoms_ref[...].astype(F32)
    geo_ref[4 * slots : 5 * slots, :] = jnp.broadcast_to(cot_ref[...], atoms_ref.shape)
    quarter = 128 // parts
    lane_part = iota((rows, 128), 1) // quarter
    for group in range(groups):
        members = min(parts, COMPONENTS - group * parts)
        chosen = dot_nn(onehot, h_ref[:, group * parts * 128 : (group * parts + members) * 128])
        blocks = []
        for part in range(parts):
            total = jnp.zeros((rows, 128), F32)
            for i in range(members):
                source = chosen[:, i * 128 : (i + 1) * 128]
                shift = ((i - part) * quarter) % 128
                if shift:
                    source = pltpu.roll(source, shift, 1)
                total = jnp.where(lane_part == i, source, total)
            blocks.append(total.reshape(n_slab, hslot, 128))
        stacked = jnp.stack(blocks, axis=1).reshape(n_slab * parts * hslot, 128)
        out_ref[:, group * 128 : (group + 1) * 128] = stacked.astype(BF)


def unpack_kernel(parts, hslot, recv_ref, turned_ref, out_hbm, out_ref, sems):
    turned = turned_ref[...]
    rows = turned.shape[1]
    n_slab = rows // hslot
    quarter = 128 // parts
    lane_part = iota((rows, 128), 1) // quarter
    groups = -(-COMPONENTS // parts)
    copies = []
    for group in range(groups):
        members = min(parts, COMPONENTS - group * parts)
        got = recv_ref[:, group * 128 : (group + 1) * 128].astype(F32)
        got = got.reshape(n_slab, parts, hslot, 128)
        pieces = [got[:, part].reshape(rows, 128) for part in range(parts)]
        placed = []
        for i in range(members):
            total = jnp.zeros((rows, 128), F32)
            for part in range(parts):
                shift = ((part - i) * quarter) % 128
                source = pltpu.roll(pieces[part], shift, 1) if shift else pieces[part]
                total = jnp.where(lane_part == part, source, total)
            placed.append(total.astype(BF))
        lanes = slice(group * parts * 128, (group * parts + members) * 128)
        out_ref[:, lanes] = dot_nn(turned, jnp.concatenate(placed, axis=1))
        copy = pltpu.make_async_copy(out_ref.at[:, lanes], out_hbm.at[:, lanes], sems.at[group])
        copy.start()
        copies.append(copy)
    for copy in copies:
        copy.wait()


def basis_kernel(
    parts, orders, slots, probes,
    me_ref, *refs,
):
    blocks = refs[:parts]
    y_all, cot_out, atoms_out, b_all, geo = refs[parts:]
    me = me_ref[0]
    for j in range(parts):
        at = pl.multiple_of((me ^ j) * probes, 128)
        geo[:, pl.ds(at, probes)] = blocks[j][...]
    xo, yo, zo = (geo[i * slots : (i + 1) * slots, :] for i in range(3))
    length = jnp.sqrt(xo * xo + yo * yo + zo * zo)
    angle = jnp.pi * length / cutoff_radius
    sine, cosine = jnp.sin(angle), jnp.cos(angle)
    scale = (2.0 / cutoff_radius) ** 0.5 * (0.5 * (cosine + 1.0)) / length
    before, now = jnp.zeros_like(sine), sine
    high, low = [], []
    for _n in range(orders):
        one, two = split(now * scale)
        high.append(one.astype(F32))
        low.append(two.astype(F32))
        before, now = now, 2.0 * cosine * now - before
    size = orders * slots
    top = jnp.concatenate(high, axis=0).astype(BF)
    b_all[0:size, :] = top
    b_all[size : 2 * size, :] = top
    b_all[2 * size : 3 * size, :] = jnp.concatenate(low, axis=0).astype(BF)
    unit = (xo / length, yo / length, zo / length)
    for index, row in enumerate(harmonic_rows(*unit)):
        row = row.astype(BF).astype(F32)
        for slot in range(slots):
            y_all[slot, index : index + 1, :] = row[slot : slot + 1, :]
    cot_out[...] = geo[4 * slots : 5 * slots, :]
    atoms_out[...] = geo[3 * slots : 4 * slots, :].astype(jnp.int32)


def prepare_kernel(
    parts, channels, slots,
    me_ref, weight_ref, pw_ref, ow_ref, halo_ref, w_all, pw_out, own_out, turned_out,
):
    quarter = channels // parts
    orders = weight_ref.shape[0]
    me = me_ref[0]
    weights = weight_ref[...]
    w_high, w_low = split(weights)
    w_high, w_low = w_high.astype(F32), w_low.astype(F32)
    spread = []
    for source in (w_high, w_low, w_high):
        for n in range(orders):
            spread.append(jnp.broadcast_to(source[n : n + 1, :], (slots, 5 * channels)))
    spread = jnp.concatenate(spread, axis=0).astype(BF)
    row = iota((5 * quarter, 5 * channels), 0)
    wanted = row // quarter * channels + me * quarter + row % quarter
    choose = (iota((5 * quarter, 5 * channels), 1) == wanted).astype(BF)
    w_all[...] = dot_nt(choose, spread)
    p_high, p_low = split(pw_ref[...].T)
    pw_out[:, 0:channels] = p_high
    pw_out[:, channels : 2 * channels] = p_low
    own = pw_ref[pl.ds(pl.multiple_of(me * quarter, quarter), quarter), :]
    eye = iota((channels, channels), 0) == iota((channels, channels), 1)
    column = jnp.sum(jnp.where(eye, ow_ref[...], 0.0), axis=1, keepdims=True)
    own_out[0:quarter, :] = own
    own_out[quarter : quarter + channels, :] = jnp.broadcast_to(column, (channels, channels))
    n_slab, hslot = halo_ref.shape[0], halo_ref.shape[2]
    onehot = owner_onehot(halo_ref[:, 0, :].astype(F32), n_slab * hslot, turned_out.shape[0], hslot)
    turned_out[...] = onehot.astype(F32).T.astype(BF)


def radial(k, slots, w_ref, b_ref, lanes):
    weights = w_ref[...]
    mine = jnp.where(iota(weights.shape, 1) % slots == k, weights, 0.0).astype(BF)
    return dot_nn(mine, b_ref[:, lanes])


def onehot_of(k, atoms_ref, table, lanes):
    atoms = atoms_ref[k : k + 1, lanes]
    return (iota((table, atoms.shape[1]), 0) == atoms).astype(F32).astype(BF)


def forward_kernel(
    quarter, h_ref, y_ref, atoms_ref, b_ref, w_ref, s_ref, hot_ref, r_ref, total
):
    slots, table = atoms_ref.shape[0], h_ref.shape[0]
    total[...] = jnp.zeros_like(total)
    for k in range(slots):
        hot = onehot_of(k, atoms_ref, table, slice(None))
        rad = radial(k, slots, w_ref, b_ref, slice(None))
        hot_ref[k] = hot
        r_ref[k] = rad
        got = dot_tn(h_ref[:, 0 : COMPONENTS * quarter], hot)
        acc = total[...]
        for degree in range(5):
            first, last = degree * degree, (degree + 1) ** 2
            inner = got[first * quarter : (first + 1) * quarter] * y_ref[k, first : first + 1, :]
            for m in range(first + 1, last):
                inner = inner + got[m * quarter : (m + 1) * quarter] * y_ref[k, m : m + 1, :]
            acc = acc + inner * rad[degree * quarter : (degree + 1) * quarter]
        total[...] = acc

    s_ref[...] = total[...].astype(BF)


def backward_kernel(
    parts, quarter, probes,
    me_ref, *refs,
):
    sums = refs[:parts]
    pw_ref, own_ref, cot_ref, y_ref, hot_ref, r_ref = refs[parts : parts + 6]
    grads_ref, density_ref, s_all, ds, z, acc, dens = refs[parts + 6 :]
    slots = y_ref.shape[0]
    me = me_ref[0]
    channels = parts * quarter
    for j in range(parts):
        at = pl.multiple_of((me ^ j) * quarter, quarter)
        s_all[pl.ds(at, quarter), :] = sums[j][...].astype(F32)
    given = s_all[...].astype(BF)
    pre = dot_nn(pw_ref[:, 0:channels], given) + dot_nn(pw_ref[:, channels : 2 * channels], given)
    ow = own_ref[quarter : quarter + channels, 0:1]
    sigma = 1.0 / (1.0 + jnp.exp(-pre))
    dens[...] = jnp.sum(pre * sigma * ow, axis=0, keepdims=True)
    here = pl.multiple_of(me * probes, 128)
    density_ref[...] = dens[:, pl.ds(here, probes)]
    dpre = cot_ref[0:1, :] * ow * sigma * (1.0 + pre * (1.0 - sigma))
    d_high, d_low = split(dpre)
    o_high, o_low = split(own_ref[0:quarter, :])
    ds[...] = dot_nn(o_high, d_high) + dot_nn(o_high, d_low) + dot_nn(o_low, d_high)
    acc[...] = jnp.zeros_like(acc)

    for k in range(slots):
        for degree in range(5):
            first, last = degree * degree, (degree + 1) ** 2
            weighted = ds[...] * r_ref[k, degree * quarter : (degree + 1) * quarter, :]
            for m in range(first, last):
                z[m * quarter : (m + 1) * quarter, :] = (
                    weighted * y_ref[k, m : m + 1, :]
                ).astype(BF)
        acc[...] += dot_nt(z[...], hot_ref[k])

    filled = (COMPONENTS * quarter) // 128 * 128
    grads_ref[:, 0:filled] = acc[0:filled, :].T.astype(BF)
    rest = acc[filled : COMPONENTS * quarter, :]
    space = grads_ref.shape[1] - COMPONENTS * quarter
    rest = jnp.concatenate([rest, jnp.zeros((space, rest.shape[1]), F32)], axis=0)
    grads_ref[:, filled:] = rest.T.astype(BF)


def spread_over(value, n_dom):
    blocks = {0: value}
    bit = n_dom // 2
    while bit:
        pairs = [(i, i ^ bit) for i in range(n_dom)]
        for j in list(blocks):
            blocks[j | bit] = lax.ppermute(blocks[j], "dom", pairs)
        bit //= 2
    return [blocks[j] for j in range(n_dom)]


def shards(
    atom_features,
    halo_lists,
    probe_atoms,
    offsets,
    radial_weights,
    probe_weight,
    out_weight,
    density_cotangent,
):
    n_slab = lax.axis_size("slab")
    n_dom = lax.axis_size("dom")
    atoms, feature_len = atom_features.shape
    channels = feature_len // COMPONENTS
    slots, probes = probe_atoms.shape
    hslot = halo_lists.shape[2]
    table = n_slab * n_dom * hslot
    quarter = channels // n_dom
    orders = radial_weights.shape[0]
    slab_probes = n_dom * probes
    packed = -(-COMPONENTS // n_dom) * 128
    me = lax.axis_index("dom").astype(jnp.int32).reshape(1)
    groups = -(-COMPONENTS // n_dom)
    wide = pltpu.CompilerParams(vmem_limit_bytes=56 * 2**20)
    narrow = pltpu.CompilerParams(vmem_limit_bytes=(16 if table <= 256 else 56) * 2**20)
    vmem = pl.BlockSpec(memory_space=pltpu.VMEM)
    smem = pl.BlockSpec(memory_space=pltpu.SMEM)
    any_space = pl.BlockSpec(memory_space=pl.ANY)

    send, geometry = pl.pallas_call(
        functools.partial(pack_kernel, n_dom),
        in_specs=[any_space] * 5,
        out_specs=[vmem, vmem],
        out_shape=[
            jax.ShapeDtypeStruct((table, packed), BF),
            jax.ShapeDtypeStruct((5 * slots, probes), F32),
        ],
        scratch_shapes=[
            pltpu.VMEM(atom_features.shape, BF),
            pltpu.VMEM(halo_lists.shape, jnp.int32),
            pltpu.VMEM(offsets.shape, F32),
            pltpu.VMEM(probe_atoms.shape, jnp.int32),
            pltpu.VMEM((1, probes), F32),
            pltpu.SemaphoreType.DMA((5,)),
        ],
        compiler_params=wide,
        name="pack",
    )(atom_features, halo_lists, offsets, probe_atoms, density_cotangent.reshape(1, probes))
    geo_blocks = spread_over(geometry, n_dom)
    halo = lax.all_to_all(send, ("slab", "dom"), split_axis=0, concat_axis=0, tiled=True)

    weights, mixing, readout, turned = pl.pallas_call(
        functools.partial(prepare_kernel, n_dom, channels, slots),
        in_specs=[smem] + [vmem] * 4,
        out_specs=[vmem] * 4,
        out_shape=[
            jax.ShapeDtypeStruct((5 * quarter, 3 * orders * slots), F32),
            jax.ShapeDtypeStruct((channels, 2 * channels), BF),
            jax.ShapeDtypeStruct((quarter + channels, channels), F32),
            jax.ShapeDtypeStruct((atoms, n_slab * hslot), BF),
        ],
        compiler_params=narrow,
        name="prepare",
    )(me, radial_weights, probe_weight, out_weight.reshape(1, channels), halo_lists)

    y_all, cot, listed, basis = pl.pallas_call(
        functools.partial(basis_kernel, n_dom, orders, slots, probes),
        in_specs=[smem] + [vmem] * n_dom,
        out_specs=[vmem] * 4,
        scratch_shapes=[pltpu.VMEM((5 * slots, slab_probes), F32)],
        out_shape=[
            jax.ShapeDtypeStruct((slots, 32, slab_probes), F32),
            jax.ShapeDtypeStruct((slots, slab_probes), F32),
            jax.ShapeDtypeStruct((slots, slab_probes), jnp.int32),
            jax.ShapeDtypeStruct((3 * orders * slots, slab_probes), BF),
        ],
        compiler_params=narrow,
        name="basis",
    )(me, *geo_blocks)

    sums, hot, r_all = pl.pallas_call(
        functools.partial(forward_kernel, quarter),
        in_specs=[vmem] * 5,
        out_specs=[vmem] * 3,
        out_shape=[
            jax.ShapeDtypeStruct((quarter, slab_probes), BF),
            jax.ShapeDtypeStruct((slots, table, slab_probes), BF),
            jax.ShapeDtypeStruct((slots, 5 * quarter, slab_probes), F32),
        ],
        scratch_shapes=[
            pltpu.VMEM((quarter, slab_probes), F32),
        ],
        compiler_params=narrow,
        name="forward",
    )(halo, y_all, listed, basis, weights)

    sum_blocks = spread_over(sums, n_dom)

    grads, density = pl.pallas_call(
        functools.partial(backward_kernel, n_dom, quarter, probes),
        in_specs=[smem] + [vmem] * (n_dom + 6),
        out_specs=[vmem, vmem],
        scratch_shapes=[
            pltpu.VMEM((channels, slab_probes), F32),
            pltpu.VMEM((quarter, slab_probes), F32),
            pltpu.VMEM((COMPONENTS * quarter, slab_probes), BF),
            pltpu.VMEM((COMPONENTS * quarter, table), F32),
            pltpu.VMEM((1, slab_probes), F32),
        ],
        out_shape=[
            jax.ShapeDtypeStruct((table, packed), BF),
            jax.ShapeDtypeStruct((1, probes), F32),
        ],
        compiler_params=narrow,
        name="backward",
    )(
        me, *sum_blocks, mixing, readout, cot, y_all,
        hot, r_all,
    )

    back = lax.all_to_all(grads, ("slab", "dom"), split_axis=0, concat_axis=0, tiled=True)
    atom_grads = pl.pallas_call(
        functools.partial(unpack_kernel, n_dom, hslot),
        in_specs=[vmem, vmem],
        out_specs=any_space,
        scratch_shapes=[
            pltpu.VMEM((atoms, feature_len), F32),
            pltpu.SemaphoreType.DMA((groups,)),
        ],
        out_shape=jax.ShapeDtypeStruct((atoms, feature_len), F32),
        compiler_params=narrow,
        name="unpack",
    )(back, turned)
    return (density.reshape(probes), atom_grads)


def solution(mesh):
    return jax.shard_map(
        shards,
        mesh=mesh,
        in_specs=(
            P(("slab", "dom"), None),
            P(None, ("slab", "dom"), None),
            P(None, ("slab", "dom")),
            P(None, None, ("slab", "dom")),
            P(),
            P(),
            P(),
            P(("slab", "dom")),
        ),
        out_specs=(P(("slab", "dom")), P(("slab", "dom"), None)),
        check_vma=False,
    )
```

```python
import functools

import jax
import jax.numpy as jnp
from jax import lax
from jax.experimental import pallas as pl
from jax.experimental.pallas import tpu as pltpu
from jax.sharding import PartitionSpec as P

cutoff_radius = 4.0
COMPONENTS = 25
BF = jnp.bfloat16
F32 = jnp.float32


def iota(shape, dim):
    return lax.broadcasted_iota(jnp.int32, shape, dim)


def dot_nn(a, b):
    return lax.dot_general(a, b, (((1,), (0,)), ((), ())), preferred_element_type=F32)


def dot_nt(a, b):
    return lax.dot_general(a, b, (((1,), (1,)), ((), ())), preferred_element_type=F32)


def dot_tn(a, b):
    return lax.dot_general(a, b, (((0,), (0,)), ((), ())), preferred_element_type=F32)


def split(value):
    high = value.astype(BF)
    return high, (value - high.astype(F32)).astype(BF)


def harmonic_rows(xc, yc, zc):
    xsq = xc * xc
    ysq = yc * yc
    zsq = zc * zc
    return [
        0.28209479 * jnp.ones_like(xc),
        0.48860251 * yc,
        0.48860251 * zc,
        0.48860251 * xc,
        1.09254843 * xc * yc,
        1.09254843 * yc * zc,
        0.31539157 * (3.0 * zsq - 1.0),
        1.09254843 * xc * zc,
        0.54627422 * (xsq - ysq),
        0.59004359 * yc * (3.0 * xsq - ysq),
        2.89061144 * xc * yc * zc,
        0.4570458 * yc * (5.0 * zsq - 1.0),
        0.37317633 * zc * (5.0 * zsq - 3.0),
        0.4570458 * xc * (5.0 * zsq - 1.0),
        1.44530572 * zc * (xsq - ysq),
        0.59004359 * xc * (xsq - 3.0 * ysq),
        2.50334294 * xc * yc * (xsq - ysq),
        1.77013077 * yc * zc * (3.0 * xsq - ysq),
        0.9461747 * xc * yc * (7.0 * zsq - 1.0),
        0.66904654 * yc * zc * (7.0 * zsq - 3.0),
        0.10578555 * (35.0 * zsq * zsq - 30.0 * zsq + 3.0),
        0.66904654 * xc * zc * (7.0 * zsq - 3.0),
        0.47308735 * (xsq - ysq) * (7.0 * zsq - 1.0),
        1.77013077 * xc * zc * (xsq - 3.0 * ysq),
        0.62583574 * (xsq * (xsq - 3.0 * ysq) - ysq * (3.0 * xsq - ysq)),
    ]


def owner_onehot(halo, rows, atoms, hslot):
    n_slab = halo.shape[0]
    pick = (iota((rows, n_slab), 0) // hslot == iota((rows, n_slab), 1)).astype(BF)
    spread = dot_nn(pick, halo.astype(BF))
    mine = iota((rows, hslot), 0) % hslot == iota((rows, hslot), 1)
    column = jnp.sum(jnp.where(mine, spread, 0.0), axis=1, keepdims=True).astype(jnp.int32)
    return (iota((rows, atoms), 1) == column).astype(BF)


def pack_kernel(
    parts,
    h_hbm, halo_hbm, off_hbm, atoms_hbm, cot_hbm,
    out_ref, geo_ref,
    h_ref, halo_ref, off_ref, atoms_ref, cot_ref, sems,
):
    groups = -(-COMPONENTS // parts)
    pairs = [
        (halo_hbm, halo_ref), (h_hbm, h_ref), (off_hbm, off_ref), (atoms_hbm, atoms_ref), (cot_hbm, cot_ref)
    ]
    copies = [
        pltpu.make_async_copy(source, target, sems.at[i]) for i, (source, target) in enumerate(pairs)
    ]
    for copy in copies:
        copy.start()
    copies[0].wait()
    n_slab, hslot = halo_ref.shape[0], halo_ref.shape[2]
    rows = n_slab * hslot
    onehot = owner_onehot(halo_ref[:, 0, :].astype(F32), rows, h_ref.shape[0], hslot)
    for copy in copies[1:]:
        copy.wait()
    slots = atoms_ref.shape[0]
    for i in range(3):
        geo_ref[i * slots : (i + 1) * slots, :] = off_ref[i]
    geo_ref[3 * slots : 4 * slots, :] = atoms_ref[...].astype(F32)
    geo_ref[4 * slots : 5 * slots, :] = jnp.broadcast_to(cot_ref[...], atoms_ref.shape)
    quarter = 128 // parts
    lane_part = iota((rows, 128), 1) // quarter
    for group in range(groups):
        members = min(parts, COMPONENTS - group * parts)
        chosen = dot_nn(onehot, h_ref[:, group * parts * 128 : (group * parts + members) * 128])
        blocks = []
        for part in range(parts):
            total = jnp.zeros((rows, 128), F32)
            for i in range(members):
                source = chosen[:, i * 128 : (i + 1) * 128]
                shift = ((i - part) * quarter) % 128
                if shift:
                    source = pltpu.roll(source, shift, 1)
                total = jnp.where(lane_part == i, source, total)
            blocks.append(total.reshape(n_slab, hslot, 128))
        stacked = jnp.stack(blocks, axis=1).reshape(n_slab * parts * hslot, 128)
        out_ref[:, group * 128 : (group + 1) * 128] = stacked.astype(BF)


def unpack_kernel(parts, hslot, recv_ref, turned_ref, out_hbm, out_ref, sems):
    turned = turned_ref[...]
    rows = turned.shape[1]
    n_slab = rows // hslot
    quarter = 128 // parts
    lane_part = iota((rows, 128), 1) // quarter
    groups = -(-COMPONENTS // parts)
    copies = []
    for group in range(groups):
        members = min(parts, COMPONENTS - group * parts)
        got = recv_ref[:, group * 128 : (group + 1) * 128].astype(F32)
        got = got.reshape(n_slab, parts, hslot, 128)
        pieces = [got[:, part].reshape(rows, 128) for part in range(parts)]
        placed = []
        for i in range(members):
            total = jnp.zeros((rows, 128), F32)
            for part in range(parts):
                shift = ((part - i) * quarter) % 128
                source = pltpu.roll(pieces[part], shift, 1) if shift else pieces[part]
                total = jnp.where(lane_part == part, source, total)
            placed.append(total.astype(BF))
        lanes = slice(group * parts * 128, (group * parts + members) * 128)
        out_ref[:, lanes] = dot_nn(turned, jnp.concatenate(placed, axis=1))
        copy = pltpu.make_async_copy(out_ref.at[:, lanes], out_hbm.at[:, lanes], sems.at[group])
        copy.start()
        copies.append(copy)
    for copy in copies:
        copy.wait()


def basis_kernel(
    parts, orders, slots, probes,
    me_ref, *refs,
):
    blocks = refs[:parts]
    y_all, cot_out, atoms_out, b_all, geo = refs[parts:]
    me = me_ref[0]
    for j in range(parts):
        at = pl.multiple_of((me ^ j) * probes, 128)
        geo[:, pl.ds(at, probes)] = blocks[j][...]
    xo, yo, zo = (geo[i * slots : (i + 1) * slots, :] for i in range(3))
    length = jnp.sqrt(xo * xo + yo * yo + zo * zo)
    angle = jnp.pi * length / cutoff_radius
    sine, cosine = jnp.sin(angle), jnp.cos(angle)
    scale = (2.0 / cutoff_radius) ** 0.5 * (0.5 * (cosine + 1.0)) / length
    before, now = jnp.zeros_like(sine), sine
    high, low = [], []
    for _n in range(orders):
        one, two = split(now * scale)
        high.append(one.astype(F32))
        low.append(two.astype(F32))
        before, now = now, 2.0 * cosine * now - before
    size = orders * slots
    top = jnp.concatenate(high, axis=0).astype(BF)
    b_all[0:size, :] = top
    b_all[size : 2 * size, :] = top
    b_all[2 * size : 3 * size, :] = jnp.concatenate(low, axis=0).astype(BF)
    unit = (xo / length, yo / length, zo / length)
    for index, row in enumerate(harmonic_rows(*unit)):
        row = row.astype(BF).astype(F32)
        for slot in range(slots):
            y_all[slot, index : index + 1, :] = row[slot : slot + 1, :]
    cot_out[...] = geo[4 * slots : 5 * slots, :]
    atoms_out[...] = geo[3 * slots : 4 * slots, :].astype(jnp.int32)


def prepare_kernel(
    parts, channels, slots,
    me_ref, weight_ref, pw_ref, ow_ref, halo_ref, w_all, pw_out, own_out, turned_out,
):
    quarter = channels // parts
    orders = weight_ref.shape[0]
    me = me_ref[0]
    weights = weight_ref[...]
    w_high, w_low = split(weights)
    w_high, w_low = w_high.astype(F32), w_low.astype(F32)
    spread = []
    for source in (w_high, w_low, w_high):
        for n in range(orders):
            spread.append(jnp.broadcast_to(source[n : n + 1, :], (slots, 5 * channels)))
    spread = jnp.concatenate(spread, axis=0).astype(BF)
    row = iota((5 * quarter, 5 * channels), 0)
    wanted = row // quarter * channels + me * quarter + row % quarter
    choose = (iota((5 * quarter, 5 * channels), 1) == wanted).astype(BF)
    w_all[...] = dot_nt(choose, spread)
    p_high, p_low = split(pw_ref[...].T)
    pw_out[:, 0:channels] = p_high
    pw_out[:, channels : 2 * channels] = p_low
    own = pw_ref[pl.ds(pl.multiple_of(me * quarter, quarter), quarter), :]
    eye = iota((channels, channels), 0) == iota((channels, channels), 1)
    column = jnp.sum(jnp.where(eye, ow_ref[...], 0.0), axis=1, keepdims=True)
    own_out[0:quarter, :] = own
    own_out[quarter : quarter + channels, :] = jnp.broadcast_to(column, (channels, channels))
    n_slab, hslot = halo_ref.shape[0], halo_ref.shape[2]
    onehot = owner_onehot(halo_ref[:, 0, :].astype(F32), n_slab * hslot, turned_out.shape[0], hslot)
    turned_out[...] = onehot.astype(F32).T.astype(BF)


def radial(k, slots, w_ref, b_ref, lanes):
    weights = w_ref[...]
    mine = jnp.where(iota(weights.shape, 1) % slots == k, weights, 0.0).astype(BF)
    return dot_nn(mine, b_ref[:, lanes])


def onehot_of(k, atoms_ref, table, lanes):
    atoms = atoms_ref[k : k + 1, lanes]
    return (iota((table, atoms.shape[1]), 0) == atoms).astype(F32).astype(BF)


def forward_kernel(
    quarter, h_ref, y_ref, atoms_ref, b_ref, w_ref, s_ref, hot_ref, r_ref, total
):
    slots, table = atoms_ref.shape[0], h_ref.shape[0]
    total[...] = jnp.zeros_like(total)
    for k in range(slots):
        hot = onehot_of(k, atoms_ref, table, slice(None))
        rad = radial(k, slots, w_ref, b_ref, slice(None))
        hot_ref[:, k * hot.shape[1] : (k + 1) * hot.shape[1]] = hot
        r_ref[k] = rad
        got = dot_tn(h_ref[:, 0 : COMPONENTS * quarter], hot)
        acc = total[...]
        for degree in range(5):
            first, last = degree * degree, (degree + 1) ** 2
            inner = got[first * quarter : (first + 1) * quarter] * y_ref[k, first : first + 1, :]
            for m in range(first + 1, last):
                inner = inner + got[m * quarter : (m + 1) * quarter] * y_ref[k, m : m + 1, :]
            acc = acc + inner * rad[degree * quarter : (degree + 1) * quarter]
        total[...] = acc

    s_ref[...] = total[...].astype(BF)


def backward_kernel(
    parts, quarter, probes,
    me_ref, *refs,
):
    sums = refs[:parts]
    pw_ref, own_ref, cot_ref, y_ref, hot_ref, r_ref = refs[parts : parts + 6]
    grads_ref, density_ref, s_all, ds, z, acc, dens = refs[parts + 6 :]
    slots, width = y_ref.shape[0], y_ref.shape[2]
    me = me_ref[0]
    channels = parts * quarter
    for j in range(parts):
        at = pl.multiple_of((me ^ j) * quarter, quarter)
        s_all[pl.ds(at, quarter), :] = sums[j][...].astype(F32)
    given = s_all[...].astype(BF)
    pre = dot_nn(pw_ref[:, 0:channels], given) + dot_nn(pw_ref[:, channels : 2 * channels], given)
    ow = own_ref[quarter : quarter + channels, 0:1]
    sigma = 1.0 / (1.0 + jnp.exp(-pre))
    dens[...] = jnp.sum(pre * sigma * ow, axis=0, keepdims=True)
    here = pl.multiple_of(me * probes, 128)
    density_ref[...] = dens[:, pl.ds(here, probes)]
    dpre = cot_ref[0:1, :] * ow * sigma * (1.0 + pre * (1.0 - sigma))
    d_high, d_low = split(dpre)
    o_high, o_low = split(own_ref[0:quarter, :])
    ds[...] = dot_nn(o_high, d_high) + dot_nn(o_high, d_low) + dot_nn(o_low, d_high)
    acc[...] = jnp.zeros_like(acc)

    for k in range(slots):
        for degree in range(5):
            first, last = degree * degree, (degree + 1) ** 2
            weighted = ds[...] * r_ref[k, degree * quarter : (degree + 1) * quarter, :]
            for m in range(first, last):
                z[m * quarter : (m + 1) * quarter, k % 2 * width : (k % 2 + 1) * width] = (
                    weighted * y_ref[k, m : m + 1, :]
                ).astype(BF)
        if k % 2 == 1:
            acc[...] += dot_nt(z[...], hot_ref[:, (k - 1) * width : (k + 1) * width])

    filled = (COMPONENTS * quarter) // 128 * 128
    grads_ref[:, 0:filled] = acc[0:filled, :].T.astype(BF)
    rest = acc[filled : COMPONENTS * quarter, :]
    space = grads_ref.shape[1] - COMPONENTS * quarter
    rest = jnp.concatenate([rest, jnp.zeros((space, rest.shape[1]), F32)], axis=0)
    grads_ref[:, filled:] = rest.T.astype(BF)


def spread_over(value, n_dom):
    blocks = {0: value}
    bit = n_dom // 2
    while bit:
        pairs = [(i, i ^ bit) for i in range(n_dom)]
        for j in list(blocks):
            blocks[j | bit] = lax.ppermute(blocks[j], "dom", pairs)
        bit //= 2
    return [blocks[j] for j in range(n_dom)]


def shards(
    atom_features,
    halo_lists,
    probe_atoms,
    offsets,
    radial_weights,
    probe_weight,
    out_weight,
    density_cotangent,
):
    n_slab = lax.axis_size("slab")
    n_dom = lax.axis_size("dom")
    atoms, feature_len = atom_features.shape
    channels = feature_len // COMPONENTS
    slots, probes = probe_atoms.shape
    hslot = halo_lists.shape[2]
    table = n_slab * n_dom * hslot
    quarter = channels // n_dom
    orders = radial_weights.shape[0]
    slab_probes = n_dom * probes
    packed = -(-COMPONENTS // n_dom) * 128
    me = lax.axis_index("dom").astype(jnp.int32).reshape(1)
    groups = -(-COMPONENTS // n_dom)
    wide = pltpu.CompilerParams(vmem_limit_bytes=56 * 2**20)
    narrow = pltpu.CompilerParams(vmem_limit_bytes=(28 if table <= 256 else 56) * 2**20)
    vmem = pl.BlockSpec(memory_space=pltpu.VMEM)
    smem = pl.BlockSpec(memory_space=pltpu.SMEM)
    any_space = pl.BlockSpec(memory_space=pl.ANY)

    send, geometry = pl.pallas_call(
        functools.partial(pack_kernel, n_dom),
        in_specs=[any_space] * 5,
        out_specs=[vmem, vmem],
        out_shape=[
            jax.ShapeDtypeStruct((table, packed), BF),
            jax.ShapeDtypeStruct((5 * slots, probes), F32),
        ],
        scratch_shapes=[
            pltpu.VMEM(atom_features.shape, BF),
            pltpu.VMEM(halo_lists.shape, jnp.int32),
            pltpu.VMEM(offsets.shape, F32),
            pltpu.VMEM(probe_atoms.shape, jnp.int32),
            pltpu.VMEM((1, probes), F32),
            pltpu.SemaphoreType.DMA((5,)),
        ],
        compiler_params=wide,
        name="pack",
    )(atom_features, halo_lists, offsets, probe_atoms, density_cotangent.reshape(1, probes))
    geo_blocks = spread_over(geometry, n_dom)
    halo = lax.all_to_all(send, ("slab", "dom"), split_axis=0, concat_axis=0, tiled=True)

    weights, mixing, readout, turned = pl.pallas_call(
        functools.partial(prepare_kernel, n_dom, channels, slots),
        in_specs=[smem] + [vmem] * 4,
        out_specs=[vmem] * 4,
        out_shape=[
            jax.ShapeDtypeStruct((5 * quarter, 3 * orders * slots), F32),
            jax.ShapeDtypeStruct((channels, 2 * channels), BF),
            jax.ShapeDtypeStruct((quarter + channels, channels), F32),
            jax.ShapeDtypeStruct((atoms, n_slab * hslot), BF),
        ],
        compiler_params=narrow,
        name="prepare",
    )(me, radial_weights, probe_weight, out_weight.reshape(1, channels), halo_lists)

    y_all, cot, listed, basis = pl.pallas_call(
        functools.partial(basis_kernel, n_dom, orders, slots, probes),
        in_specs=[smem] + [vmem] * n_dom,
        out_specs=[vmem] * 4,
        scratch_shapes=[pltpu.VMEM((5 * slots, slab_probes), F32)],
        out_shape=[
            jax.ShapeDtypeStruct((slots, 32, slab_probes), F32),
            jax.ShapeDtypeStruct((slots, slab_probes), F32),
            jax.ShapeDtypeStruct((slots, slab_probes), jnp.int32),
            jax.ShapeDtypeStruct((3 * orders * slots, slab_probes), BF),
        ],
        compiler_params=narrow,
        name="basis",
    )(me, *geo_blocks)

    sums, hot, r_all = pl.pallas_call(
        functools.partial(forward_kernel, quarter),
        in_specs=[vmem] * 5,
        out_specs=[vmem] * 3,
        out_shape=[
            jax.ShapeDtypeStruct((quarter, slab_probes), BF),
            jax.ShapeDtypeStruct((table, slots * slab_probes), BF),
            jax.ShapeDtypeStruct((slots, 5 * quarter, slab_probes), F32),
        ],
        scratch_shapes=[
            pltpu.VMEM((quarter, slab_probes), F32),
        ],
        compiler_params=narrow,
        name="forward",
    )(halo, y_all, listed, basis, weights)

    sum_blocks = spread_over(sums, n_dom)

    grads, density = pl.pallas_call(
        functools.partial(backward_kernel, n_dom, quarter, probes),
        in_specs=[smem] + [vmem] * (n_dom + 6),
        out_specs=[vmem, vmem],
        scratch_shapes=[
            pltpu.VMEM((channels, slab_probes), F32),
            pltpu.VMEM((quarter, slab_probes), F32),
            pltpu.VMEM((COMPONENTS * quarter, 2 * slab_probes), BF),
            pltpu.VMEM((COMPONENTS * quarter, table), F32),
            pltpu.VMEM((1, slab_probes), F32),
        ],
        out_shape=[
            jax.ShapeDtypeStruct((table, packed), BF),
            jax.ShapeDtypeStruct((1, probes), F32),
        ],
        compiler_params=narrow,
        name="backward",
    )(
        me, *sum_blocks, mixing, readout, cot, y_all,
        hot, r_all,
    )

    back = lax.all_to_all(grads, ("slab", "dom"), split_axis=0, concat_axis=0, tiled=True)
    atom_grads = pl.pallas_call(
        functools.partial(unpack_kernel, n_dom, hslot),
        in_specs=[vmem, vmem],
        out_specs=any_space,
        scratch_shapes=[
            pltpu.VMEM((atoms, feature_len), F32),
            pltpu.SemaphoreType.DMA((groups,)),
        ],
        out_shape=jax.ShapeDtypeStruct((atoms, feature_len), F32),
        compiler_params=narrow,
        name="unpack",
    )(back, turned)
    return (density.reshape(probes), atom_grads)


def solution(mesh):
    return jax.shard_map(
        shards,
        mesh=mesh,
        in_specs=(
            P(("slab", "dom"), None),
            P(None, ("slab", "dom"), None),
            P(None, ("slab", "dom")),
            P(None, None, ("slab", "dom")),
            P(),
            P(),
            P(),
            P(("slab", "dom")),
        ),
        out_specs=(P(("slab", "dom")), P(("slab", "dom"), None)),
        check_vma=False,
    )
```
